32 devices in a mesh: dom: 2 (over core), gx: 4 (over y, x), gy: 4 (over z).
Axes of the slice: x: 2, y: 2, z: 4, core: 2. Of those that a mesh axis runs over, the one named last changes fastest.
Arguments:
- wind: float32 [2, 3, 64, 64, 128], P('dom', None, 'gx', 'gy'), may hold values from -6 to 6
- adjoint: float32 [2, 4, 64, 64, 128], P('dom', None, 'gx', 'gy'), may hold values from -6 to 6
- turbines: int32 [64, 64, 128], P('gx', 'gy'), may hold values 0 or 1
- fringe_range: int32 [2], replicated, may hold values from 8 to 63, as said below
Outputs:
- earlier: float32 [2, 4, 64, 64, 128], P('dom', None, 'gx', 'gy')
The draws below stay inside these ranges and needn't reach their ends.
Inputs may be any that keep to these rules, and one draw needn't show every extreme that they name: `fringe_range`: element 0 is the first streamwise cell of the fringe, the last cell 64 - 1 of the domain, and element 1 its length in cells, from 8 to 16; the fringe wraps around the periodic streamwise dimension.
All inputs are finite; a program needn't handle non-finite values. No bound on the sum of `turbines` on one device may be relied on, other than what follows from the above.
Results may differ from the reference program's by a relative error of at most 0.00002.
Values sent between devices are 32-bit elements; how exact they have to be, the bound alone decides.
A program may use at most 64 MiB of HBM per device.

```python
import math
import jax
import jax.numpy as jnp

STEPS = 2
NX = 64
NY = 64
NZ = 128


def draw_fringe_range(key, part):
    span_key = jax.random.fold_in(key, 17)
    fringe_span = jax.random.randint(span_key, (1,), NX // 8, NX // 4 + 1)
    first_cell = jnp.full((1,), NX - 1, dtype=jnp.int32)
    return jnp.concatenate([first_cell, fringe_span.astype(jnp.int32)]).astype(jnp.int32)


def set_ends(entries, key, least, top_value):
    shape = entries.shape
    spot = [jax.random.randint(jax.random.fold_in(key, axis), (), 0, shape[axis]) for axis in range(len(shape))]
    entries = entries.at[tuple(spot)].set(least)
    longest = shape.index(max(shape))
    spot[longest] = (spot[longest] + 1) % shape[longest]
    return entries.at[tuple(spot)].set(top_value)


def level_of(rng, shape, cuts, least, top_value):
    def one(dim, parts):
        draws = jax.random.uniform(jax.random.fold_in(jax.random.fold_in(rng, 6), dim), (parts,), jnp.float32, least / len(cuts), top_value / len(cuts))
        return jnp.repeat(jnp.exp(draws), shape[dim] // parts).reshape((-1,) + (1,) * (len(shape) - dim - 1))

    factor_of = one(*cuts[0])
    for cut in cuts[1:]:
        factor_of = factor_of * one(*cut)
    return factor_of


def noise(rng, dims, width, reach, cuts=(), kind=jnp.bfloat16):
    factor_of = level_of(rng, dims, cuts, -0.22, 0.18) if cuts else 1.0
    result = jax.random.normal(rng, dims, jnp.float32) * width * factor_of
    return jnp.minimum(jnp.maximum(result, -reach), reach).astype(kind)


def setup_inputs(seed: int = 0) -> dict:
    key_of = jax.random.split(jax.random.key(seed), 5)
    wind = noise(key_of[0], (2, 3, NX, NY, NZ), 1.0, 6.0, ((0, 2), (2, 4), (3, 4)), jnp.float32)
    adjoint = noise(key_of[1], (2, 4, NX, NY, NZ), 1.0, 6.0, ((0, 2), (2, 4), (3, 4)), jnp.float32)
    turbines = set_ends((jax.random.randint(key_of[2], (NX, NY, NZ), 0, 8) < 1).astype(jnp.int32), jax.random.fold_in(key_of[2], 1), 0, 1)
    fringe_range = draw_fringe_range(jax.random.fold_in(key_of[4], 71), 0)
    return {"wind": wind, "adjoint": adjoint, "turbines": turbines, "fringe_range": fringe_range}


DT = 0.1
SMAG = 0.1
SOUND_SQ = 4.0
DRAG = 1.0
RATE = 3.0

def crop_xy(field, margin):
    if margin == 0:
        return field
    return field[..., margin:field.shape[-3] - margin, margin:field.shape[-2] - margin, :]

def pad_z(field):
    return jnp.pad(field, [(0, 0)] * (field.ndim - 1) + [(1, 1)])

def diff_x(field):
    return 0.5 * (field[..., 2:, 1:-1, :] - field[..., :-2, 1:-1, :])

def diff_y(field):
    return 0.5 * (field[..., 1:-1, 2:, :] - field[..., 1:-1, :-2, :])

def diff_z(field):
    padded = crop_xy(pad_z(field), 1)
    return 0.5 * (padded[..., 2:] - padded[..., :-2])

def eddy(wind_ext):
    grads = (diff_x(wind_ext), diff_y(wind_ext), diff_z(wind_ext))
    strain_sq = jnp.zeros_like(grads[0][0])
    for first in range(3):
        for second in range(3):
            strain = 0.5 * (grads[first][second] + grads[second][first])
            strain_sq = strain_sq + strain * strain
    return SMAG * jnp.sqrt(2.0 * strain_sq)

def spread(field, viscosity):
    centre = crop_xy(field, 1)
    visc_mid = crop_xy(viscosity, 1)
    flux_xp = (viscosity[..., 2:, 1:-1, :] + visc_mid) * 0.5 * (field[..., 2:, 1:-1, :] - centre)
    flux_xm = (visc_mid + viscosity[..., :-2, 1:-1, :]) * 0.5 * (centre - field[..., :-2, 1:-1, :])
    flux_yp = (viscosity[..., 1:-1, 2:, :] + visc_mid) * 0.5 * (field[..., 1:-1, 2:, :] - centre)
    flux_ym = (visc_mid + viscosity[..., 1:-1, :-2, :]) * 0.5 * (centre - field[..., 1:-1, :-2, :])
    visc_pad = pad_z(visc_mid)
    field_pad = pad_z(centre)
    flux_zp = (visc_pad[..., 2:] + visc_mid) * 0.5 * (field_pad[..., 2:] - centre)
    flux_zm = (visc_mid + visc_pad[..., :-2]) * 0.5 * (centre - field_pad[..., :-2])
    return flux_xp - flux_xm + flux_yp - flux_ym + flux_zp - flux_zm

def tendency(adjoint_ext, wind_here, viscosity, drag_cells):
    along_x = diff_x(adjoint_ext)
    along_y = diff_y(adjoint_ext)
    along_z = diff_z(adjoint_ext)
    advection = wind_here[0] * along_x + wind_here[1] * along_y + wind_here[2] * along_z
    diffusion = spread(adjoint_ext[:3], viscosity)
    wind_speed = jnp.sqrt(wind_here[0] * wind_here[0] + wind_here[1] * wind_here[1] + wind_here[2] * wind_here[2])
    centre = crop_xy(adjoint_ext, 1)
    acoustic = SOUND_SQ * jnp.stack([along_x[3], along_y[3], along_z[3]], 0)
    velocity = advection[:3] + diffusion + acoustic - DRAG * drag_cells * wind_speed * centre[:3]
    pressure = advection[3] + along_x[0] + along_y[1] + along_z[2]
    return (centre, jnp.concatenate([velocity, pressure[None]], 0))

def ramp(position, fringe_range, length_total):
    offset = jnp.mod(position - fringe_range[0], length_total)
    fringe_width = fringe_range[1]
    fringe_phase = math.pi * (offset.astype(jnp.float32) + 0.5) / fringe_width.astype(jnp.float32)
    sine = jnp.sin(fringe_phase)
    return jnp.where(offset < fringe_width, RATE * sine * sine, 0.0).astype(jnp.float32)

def wrap_xy(field, extent):
    return jnp.pad(field, [(0, 0)] * (field.ndim - 3) + [(extent, extent), (extent, extent), (0, 0)], mode='wrap')

def reference(wind, adjoint, turbines, fringe_range):
    fringe_rates = ramp(jnp.arange(NX, dtype=jnp.int32), fringe_range, NX)[:, None, None]
    drag_main = turbines.astype(jnp.float32)
    nothing = jnp.zeros_like(drag_main)
    viscosity = [eddy(wrap_xy(wind[domain], 1)) for domain in range(2)]
    states = [adjoint[0], adjoint[1]]
    for step in range(STEPS):
        updated = []
        forcing = None
        for domain in range(2):
            drag_cells = drag_main if domain == 0 else nothing
            centre, rate_term = tendency(wrap_xy(states[domain], 1), wind[domain], wrap_xy(viscosity[domain], 1), drag_cells)
            if domain == 0:
                forcing = jnp.concatenate([fringe_rates * centre[:3], jnp.zeros_like(centre[3:])], 0)
                updated.append(centre + DT * (rate_term - forcing))
            else:
                updated.append(centre + DT * (rate_term + forcing))
        states = updated
    return jnp.stack(states)
```

```python
import functools
import math

import jax
import jax.numpy as jnp
from jax import lax
from jax.experimental import pallas as pl
from jax.experimental.pallas import tpu as pltpu
from jax.sharding import PartitionSpec as P

DT = 0.1
SMAG = 0.1
SOUND_SQ = 4.0
DRAG = 1.0
RATE = 3.0
H = 0.5 * DT
GROUP = 2


def shifted_z(field):
    depth = field.shape[-1]
    lane = lax.broadcasted_iota(jnp.int32, field.shape, 1)
    after = jnp.where(lane == depth - 1, 0.0, pltpu.roll(field, depth - 1, 1))
    before = jnp.where(lane == 0, 0.0, pltpu.roll(field, 1, 1))
    return after, before


def shifted_y(field, row_after, row_before):
    rows = field.shape[0]
    row = lax.broadcasted_iota(jnp.int32, field.shape, 0)
    after = jnp.where(row == rows - 1, row_after, pltpu.roll(field, rows - 1, 0))
    before = jnp.where(row == 0, row_before, pltpu.roll(field, 1, 0))
    return after, before


def neighbours(ext, sides, c, x):
    here = ext[c, x + 1]
    yp, ym = shifted_y(here, sides[1, c, x], sides[0, c, x])
    zp, zm = shifted_z(here)
    return here, ext[c, x + 2], ext[c, x], yp, ym, zp, zm


def kernel(
    sizes,
    fringe,
    wind,
    wind_rows,
    adjoint,
    adjoint_rows,
    turbines,
    out,
    a_ext,
    w_ext,
    n_ext,
    b_ext,
    turb,
    coef,
    a_in,
    w_in,
    n_in,
    b_in,
    n_out,
    b_out,
    first_main,
    second_main,
    rates,
    load_sem,
    send_sem,
    recv_sem,
):
    n_gx, n_gy = sizes
    cells_x, cells_y, cells_z = turb.shape
    dom, gx, gy = (lax.axis_index(a) for a in ("dom", "gx", "gy"))
    total = cells_x * n_gx
    reach = total // 4 - 1
    is_main = dom == 0
    in_fringe = jnp.logical_or(gx == n_gx - 1, gx * cells_x < reach)
    sends_forcing = jnp.logical_and(is_main, in_fringe)
    gets_forcing = jnp.logical_and(jnp.logical_not(is_main), in_fringe)
    up_x, down_x = lax.rem(gx + 1, n_gx), lax.rem(gx + n_gx - 1, n_gx)
    up_y, down_y = lax.rem(gy + 1, n_gy), lax.rem(gy + n_gy - 1, n_gy)
    places = ({"gx": up_x}, {"gx": down_x}, {"gy": up_y}, {"gy": down_y})
    partner = {"dom": 1 - dom}

    def remote(src, dst, slot, device):
        return pltpu.make_async_remote_copy(
            src_ref=src,
            dst_ref=dst,
            send_sem=send_sem.at[slot],
            recv_sem=recv_sem.at[slot],
            device_id=device,
            device_id_type=pl.DeviceIdType.MESH,
        )

    load_wind = pltpu.make_async_copy(wind.at[0], w_ext.at[:, pl.ds(1, cells_x)], load_sem.at[0])
    load_adjoint = pltpu.make_async_copy(
        adjoint.at[0], a_ext.at[:, pl.ds(1, cells_x)], load_sem.at[1]
    )
    load_turbines = pltpu.make_async_copy(turbines, turb, load_sem.at[2])
    load_wind.start()

    barrier = pltpu.get_barrier_semaphore()
    for place in places + (partner,):
        pl.semaphore_signal(
            barrier, inc=1, device_id=place, device_id_type=pl.DeviceIdType.MESH
        )
    load_adjoint.start()
    load_turbines.start()

    position = gx * cells_x + lax.broadcasted_iota(jnp.int32, (cells_x, cells_z), 0)
    offset = position - fringe[0]
    offset = jnp.where(offset < 0, offset + total, offset)
    phase = math.pi * (offset.astype(jnp.float32) + 0.5) / fringe[1].astype(jnp.float32)
    sine = jnp.sin(phase)
    sign = jnp.where(is_main, -DT, DT)
    rates[...] = jnp.where(offset < fringe[1], sign * (RATE * sine * sine), 0.0)

    pl.semaphore_wait(barrier, len(places) + 1)

    def exchange(slot, ext, x_src, y_src, sides, lead):
        last, first = x_src
        pieces = (
            remote(last, ext.at[:, 0] if lead else ext.at[0], slot, places[0]),
            remote(
                first,
                ext.at[:, cells_x + 1] if lead else ext.at[cells_x + 1],
                slot + 1,
                places[1],
            ),
            remote(y_src[0], sides.at[0], slot + 2, places[2]),
            remote(y_src[1], sides.at[1], slot + 3, places[3]),
        )
        for k in (2, 3, 0, 1):
            pieces[k].start()
        return pieces

    wind_copies = exchange(
        0,
        w_ext,
        (wind.at[0, :, cells_x - 1], wind.at[0, :, 0]),
        (wind_rows.at[:, :, cells_y - 1], wind_rows.at[:, :, 0]),
        w_in,
        True,
    )
    adjoint_copies = exchange(
        4,
        a_ext,
        (adjoint.at[0, :, cells_x - 1], adjoint.at[0, :, 0]),
        (adjoint_rows.at[:, :, cells_y - 1], adjoint_rows.at[:, :, 0]),
        a_in,
        True,
    )
    first_forcing = remote(adjoint.at[0, pl.ds(0, 3)], first_main, 16, partner)

    @pl.when(sends_forcing)
    def _():
        first_forcing.start()

    load_wind.wait()
    for piece in wind_copies:
        piece.wait_recv()

    def viscosity(x):
        grads = []
        for c in range(3):
            _, xp, xm, yp, ym, zp, zm = neighbours(w_ext, w_in, c, x)
            grads.append((xp - xm, yp - ym, zp - zm))
        own = sum(grads[k][k] * grads[k][k] for k in range(3))
        xy = grads[0][1] + grads[1][0]
        xz = grads[0][2] + grads[2][0]
        yz = grads[1][2] + grads[2][1]
        nu = (0.5 * SMAG) * jnp.sqrt(2.0 * own + (xy * xy + xz * xz + yz * yz))
        n_ext[x + 1] = nu
        n_out[0, x] = nu[cells_y - 1 :]
        n_out[1, x] = nu[:1]

    def for_slabs(body):
        def step(i, carry):
            for k in range(GROUP):
                body(i * GROUP + k)
            return carry

        lax.fori_loop(0, cells_x // GROUP, step, 0)

    for_slabs(viscosity)
    viscosity_copies = exchange(
        8,
        n_ext,
        (n_ext.at[cells_x], n_ext.at[1]),
        (n_out.at[0], n_out.at[1]),
        n_in,
        False,
    )
    load_turbines.wait()
    load_adjoint.wait()
    for piece in adjoint_copies + viscosity_copies:
        piece.wait_recv()

    @pl.when(gets_forcing)
    def _():
        first_forcing.wait_recv()

    drag_scale = jnp.where(is_main, DT * DRAG, 0.0)

    def coefficients(x):
        nu, u, v, w = n_ext[x + 1], w_ext[0, x + 1], w_ext[1, x + 1], w_ext[2, x + 1]
        nxp, nxm = n_ext[x + 2] + nu, n_ext[x] + nu
        nyp, nym = shifted_y(nu, n_in[1, x], n_in[0, x])
        nzp, nzm = shifted_z(nu)
        nyp, nym, nzp, nzm = nyp + nu, nym + nu, nzp + nu, nzm + nu
        speed = jnp.sqrt(u * u + v * v + w * w)
        drag = drag_scale * turb[x].astype(jnp.float32) * speed
        around = (nxp + nxm) + (nyp + nym) + (nzp + nzm)
        return (
            1.0 - H * around - drag,
            H * (nxp + u),
            H * (nxm - u),
            H * (nyp + v),
            H * (nym - v),
            H * (nzp + w),
            H * (nzm - w),
        )

    def advance(ext, sides, main, weights, x):
        u, v, w = w_ext[0, x + 1], w_ext[1, x + 1], w_ext[2, x + 1]
        p, pxp, pxm, pyp, pym, pzp, pzm = neighbours(ext, sides, 3, x)
        slopes = (pxp - pxm, pyp - pym, pzp - pzm)
        gain = u * slopes[0] + v * slopes[1] + w * slopes[2]
        rate = rates[pl.ds(x, 1)]
        results = []
        for c in range(3):
            stencil = neighbours(ext, sides, c, x)
            gain = gain + (stencil[1 + 2 * c] - stencil[2 + 2 * c])
            new = sum(k * f for k, f in zip(weights, stencil))
            source = jnp.where(gets_forcing, main[c, x], stencil[0])
            results.append(new + (SOUND_SQ * H) * slopes[c] + rate * source)
        results.append(p + H * gain)
        return results

    def first_step(x):
        weights = coefficients(x)
        for k, weight in enumerate(weights):
            coef[k, x] = weight
        for c, new in enumerate(advance(a_ext, a_in, first_main, weights, x)):
            b_ext[c, x + 1] = new
            b_out[0, c, x] = new[cells_y - 1 :]
            b_out[1, c, x] = new[:1]

    for_slabs(first_step)
    second_copies = exchange(
        12,
        b_ext,
        (b_ext.at[:, cells_x], b_ext.at[:, 1]),
        (b_out.at[0], b_out.at[1]),
        b_in,
        True,
    )
    second_forcing = remote(
        b_ext.at[pl.ds(0, 3), pl.ds(1, cells_x)], second_main, 17, partner
    )

    @pl.when(sends_forcing)
    def _():
        second_forcing.start()

    for piece in second_copies:
        piece.wait_recv()

    @pl.when(gets_forcing)
    def _():
        second_forcing.wait_recv()

    def second_step(x):
        weights = tuple(coef[k, x] for k in range(7))
        for c, new in enumerate(advance(b_ext, b_in, second_main, weights, x)):
            out[0, c, x] = new

    for_slabs(second_step)

    for piece in wind_copies + adjoint_copies + viscosity_copies + second_copies:
        piece.wait_send()

    @pl.when(sends_forcing)
    def _():
        first_forcing.wait_send()
        second_forcing.wait_send()


def on_device(wind, adjoint, turbines, fringe_range):
    _, _, cx, cy, cz = wind.shape
    f32 = jnp.float32
    sizes = (lax.axis_size("gx"), lax.axis_size("gy"))
    anywhere = pl.BlockSpec(memory_space=pltpu.HBM)
    return pl.pallas_call(
        functools.partial(kernel, sizes),
        out_shape=jax.ShapeDtypeStruct(adjoint.shape, f32),
        in_specs=[pl.BlockSpec(memory_space=pltpu.SMEM)] + [anywhere] * 5,
        out_specs=pl.BlockSpec(memory_space=pltpu.VMEM),
        scratch_shapes=[
            pltpu.VMEM((4, cx + 2, cy, cz), f32),
            pltpu.VMEM((3, cx + 2, cy, cz), f32),
            pltpu.VMEM((cx + 2, cy, cz), f32),
            pltpu.VMEM((4, cx + 2, cy, cz), f32),
            pltpu.VMEM((cx, cy, cz), jnp.int32),
            pltpu.VMEM((7, cx, cy, cz), f32),
            pltpu.VMEM((2, 4, cx, 1, cz), f32),
            pltpu.VMEM((2, 3, cx, 1, cz), f32),
            pltpu.VMEM((2, cx, 1, cz), f32),
            pltpu.VMEM((2, 4, cx, 1, cz), f32),
            pltpu.VMEM((2, cx, 1, cz), f32),
            pltpu.VMEM((2, 4, cx, 1, cz), f32),
            pltpu.VMEM((3, cx, cy, cz), f32),
            pltpu.VMEM((3, cx, cy, cz), f32),
            pltpu.VMEM((cx, cz), f32),
            pltpu.SemaphoreType.DMA((3,)),
            pltpu.SemaphoreType.DMA((18,)),
            pltpu.SemaphoreType.DMA((18,)),
        ],
        compiler_params=pltpu.CompilerParams(
            collective_id=0, has_side_effects=True, vmem_limit_bytes=60 * 1024 * 1024
        ),
        name="adjoint_steps",
    )(
        fringe_range,
        wind,
        wind.reshape(3, cx, cy, 1, cz),
        adjoint,
        adjoint.reshape(4, cx, cy, 1, cz),
        turbines,
    )


def solution(mesh):
    in_specs = (
        P("dom", None, "gx", "gy", None),
        P("dom", None, "gx", "gy", None),
        P("gx", "gy", None),
        P(),
    )
    out_specs = P("dom", None, "gx", "gy", None)
    return jax.shard_map(
        on_device, mesh=mesh, in_specs=in_specs, out_specs=out_specs, check_vma=False
    )
```

```python
import functools
import math

import jax
import jax.numpy as jnp
from jax import lax
from jax.experimental import pallas as pl
from jax.experimental.pallas import tpu as pltpu
from jax.sharding import PartitionSpec as P

DT = 0.1
SMAG = 0.1
SOUND_SQ = 4.0
DRAG = 1.0
RATE = 3.0
H = 0.5 * DT
GROUP = 8


def shifted_z(field):
    depth = field.shape[-1]
    lane = lax.broadcasted_iota(jnp.int32, field.shape, 1)
    after = jnp.where(lane == depth - 1, 0.0, pltpu.roll(field, depth - 1, 1))
    before = jnp.where(lane == 0, 0.0, pltpu.roll(field, 1, 1))
    return after, before


def shifted_y(field, row_after, row_before):
    rows = field.shape[0]
    row = lax.broadcasted_iota(jnp.int32, field.shape, 0)
    after = jnp.where(row == rows - 1, row_after, pltpu.roll(field, rows - 1, 0))
    before = jnp.where(row == 0, row_before, pltpu.roll(field, 1, 0))
    return after, before


def neighbours(ext, sides, c, x):
    here = ext[c, x + 1]
    yp, ym = shifted_y(here, sides[1, c, x], sides[0, c, x])
    zp, zm = shifted_z(here)
    return here, ext[c, x + 2], ext[c, x], yp, ym, zp, zm


def kernel(
    sizes,
    fringe,
    wind,
    wind_rows,
    adjoint,
    adjoint_rows,
    turbines,
    out,
    a_ext,
    w_ext,
    n_ext,
    b_ext,
    turb,
    coef,
    a_in,
    w_in,
    n_in,
    b_in,
    n_out,
    b_out,
    first_main,
    second_main,
    rates,
    load_sem,
    send_sem,
    recv_sem,
):
    n_gx, n_gy = sizes
    cells_x, cells_y, cells_z = turb.shape
    dom, gx, gy = (lax.axis_index(a) for a in ("dom", "gx", "gy"))
    total = cells_x * n_gx
    reach = total // 4 - 1
    is_main = dom == 0
    in_fringe = jnp.logical_or(gx == n_gx - 1, gx * cells_x < reach)
    sends_forcing = jnp.logical_and(is_main, in_fringe)
    gets_forcing = jnp.logical_and(jnp.logical_not(is_main), in_fringe)
    up_x, down_x = lax.rem(gx + 1, n_gx), lax.rem(gx + n_gx - 1, n_gx)
    up_y, down_y = lax.rem(gy + 1, n_gy), lax.rem(gy + n_gy - 1, n_gy)
    places = ({"gx": up_x}, {"gx": down_x}, {"gy": up_y}, {"gy": down_y})
    partner = {"dom": 1 - dom}

    def remote(src, dst, slot, device):
        return pltpu.make_async_remote_copy(
            src_ref=src,
            dst_ref=dst,
            send_sem=send_sem.at[slot],
            recv_sem=recv_sem.at[slot],
            device_id=device,
            device_id_type=pl.DeviceIdType.MESH,
        )

    load_wind = pltpu.make_async_copy(wind.at[0], w_ext.at[:, pl.ds(1, cells_x)], load_sem.at[0])
    load_adjoint = pltpu.make_async_copy(
        adjoint.at[0], a_ext.at[:, pl.ds(1, cells_x)], load_sem.at[1]
    )
    load_turbines = pltpu.make_async_copy(turbines, turb, load_sem.at[2])
    load_wind.start()

    barrier = pltpu.get_barrier_semaphore()
    for place in places + (partner,):
        pl.semaphore_signal(
            barrier, inc=1, device_id=place, device_id_type=pl.DeviceIdType.MESH
        )
    load_adjoint.start()
    load_turbines.start()

    position = gx * cells_x + lax.broadcasted_iota(jnp.int32, (cells_x, cells_z), 0)
    offset = position - fringe[0]
    offset = jnp.where(offset < 0, offset + total, offset)
    phase = math.pi * (offset.astype(jnp.float32) + 0.5) / fringe[1].astype(jnp.float32)
    sine = jnp.sin(phase)
    sign = jnp.where(is_main, -DT, DT)
    rates[...] = jnp.where(offset < fringe[1], sign * (RATE * sine * sine), 0.0)

    pl.semaphore_wait(barrier, len(places) + 1)

    def exchange(slot, ext, x_src, y_src, sides, lead):
        last, first = x_src
        pieces = (
            remote(last, ext.at[:, 0] if lead else ext.at[0], slot, places[0]),
            remote(
                first,
                ext.at[:, cells_x + 1] if lead else ext.at[cells_x + 1],
                slot + 1,
                places[1],
            ),
            remote(y_src[0], sides.at[0], slot + 2, places[2]),
            remote(y_src[1], sides.at[1], slot + 3, places[3]),
        )
        for k in (2, 3, 0, 1):
            pieces[k].start()
        return pieces

    wind_copies = exchange(
        0,
        w_ext,
        (wind.at[0, :, cells_x - 1], wind.at[0, :, 0]),
        (wind_rows.at[:, :, cells_y - 1], wind_rows.at[:, :, 0]),
        w_in,
        True,
    )
    adjoint_copies = exchange(
        4,
        a_ext,
        (adjoint.at[0, :, cells_x - 1], adjoint.at[0, :, 0]),
        (adjoint_rows.at[:, :, cells_y - 1], adjoint_rows.at[:, :, 0]),
        a_in,
        True,
    )
    first_forcing = remote(adjoint.at[0, pl.ds(0, 3)], first_main, 16, partner)

    @pl.when(sends_forcing)
    def _():
        first_forcing.start()

    load_wind.wait()
    for piece in wind_copies:
        piece.wait_recv()

    def viscosity(x):
        grads = []
        for c in range(3):
            _, xp, xm, yp, ym, zp, zm = neighbours(w_ext, w_in, c, x)
            grads.append((xp - xm, yp - ym, zp - zm))
        own = sum(grads[k][k] * grads[k][k] for k in range(3))
        xy = grads[0][1] + grads[1][0]
        xz = grads[0][2] + grads[2][0]
        yz = grads[1][2] + grads[2][1]
        nu = (0.5 * SMAG) * jnp.sqrt(2.0 * own + (xy * xy + xz * xz + yz * yz))
        n_ext[x + 1] = nu
        n_out[0, x] = nu[cells_y - 1 :]
        n_out[1, x] = nu[:1]

    def for_slabs(body):
        def step(i, carry):
            for k in range(GROUP):
                body(i * GROUP + k)
            return carry

        lax.fori_loop(0, cells_x // GROUP, step, 0)

    for_slabs(viscosity)
    viscosity_copies = exchange(
        8,
        n_ext,
        (n_ext.at[cells_x], n_ext.at[1]),
        (n_out.at[0], n_out.at[1]),
        n_in,
        False,
    )
    load_turbines.wait()
    load_adjoint.wait()
    for piece in adjoint_copies + viscosity_copies:
        piece.wait_recv()

    @pl.when(gets_forcing)
    def _():
        first_forcing.wait_recv()

    drag_scale = jnp.where(is_main, DT * DRAG, 0.0)

    def coefficients(x):
        nu, u, v, w = n_ext[x + 1], w_ext[0, x + 1], w_ext[1, x + 1], w_ext[2, x + 1]
        nxp, nxm = n_ext[x + 2] + nu, n_ext[x] + nu
        nyp, nym = shifted_y(nu, n_in[1, x], n_in[0, x])
        nzp, nzm = shifted_z(nu)
        nyp, nym, nzp, nzm = nyp + nu, nym + nu, nzp + nu, nzm + nu
        speed = jnp.sqrt(u * u + v * v + w * w)
        drag = drag_scale * turb[x].astype(jnp.float32) * speed
        around = (nxp + nxm) + (nyp + nym) + (nzp + nzm)
        return (
            1.0 - H * around - drag,
            H * (nxp + u),
            H * (nxm - u),
            H * (nyp + v),
            H * (nym - v),
            H * (nzp + w),
            H * (nzm - w),
        )

    def advance(ext, sides, main, weights, x):
        u, v, w = w_ext[0, x + 1], w_ext[1, x + 1], w_ext[2, x + 1]
        p, pxp, pxm, pyp, pym, pzp, pzm = neighbours(ext, sides, 3, x)
        slopes = (pxp - pxm, pyp - pym, pzp - pzm)
        gain = u * slopes[0] + v * slopes[1] + w * slopes[2]
        rate = rates[pl.ds(x, 1)]
        results = []
        for c in range(3):
            stencil = neighbours(ext, sides, c, x)
            gain = gain + (stencil[1 + 2 * c] - stencil[2 + 2 * c])
            new = sum(k * f for k, f in zip(weights, stencil))
            source = jnp.where(gets_forcing, main[c, x], stencil[0])
            results.append(new + (SOUND_SQ * H) * slopes[c] + rate * source)
        results.append(p + H * gain)
        return results

    def first_step(x):
        weights = coefficients(x)
        for k, weight in enumerate(weights):
            coef[k, x] = weight
        for c, new in enumerate(advance(a_ext, a_in, first_main, weights, x)):
            b_ext[c, x + 1] = new
            b_out[0, c, x] = new[cells_y - 1 :]
            b_out[1, c, x] = new[:1]

    for_slabs(first_step)
    second_copies = exchange(
        12,
        b_ext,
        (b_ext.at[:, cells_x], b_ext.at[:, 1]),
        (b_out.at[0], b_out.at[1]),
        b_in,
        True,
    )
    second_forcing = remote(
        b_ext.at[pl.ds(0, 3), pl.ds(1, cells_x)], second_main, 17, partner
    )

    @pl.when(sends_forcing)
    def _():
        second_forcing.start()

    for piece in second_copies:
        piece.wait_recv()

    @pl.when(gets_forcing)
    def _():
        second_forcing.wait_recv()

    def second_step(x):
        weights = tuple(coef[k, x] for k in range(7))
        for c, new in enumerate(advance(b_ext, b_in, second_main, weights, x)):
            out[0, c, x] = new

    for_slabs(second_step)

    for piece in wind_copies + adjoint_copies + viscosity_copies + second_copies:
        piece.wait_send()

    @pl.when(sends_forcing)
    def _():
        first_forcing.wait_send()
        second_forcing.wait_send()


def on_device(wind, adjoint, turbines, fringe_range):
    _, _, cx, cy, cz = wind.shape
    f32 = jnp.float32
    sizes = (lax.axis_size("gx"), lax.axis_size("gy"))
    anywhere = pl.BlockSpec(memory_space=pltpu.HBM)
    return pl.pallas_call(
        functools.partial(kernel, sizes),
        out_shape=pltpu.VMEM(adjoint.shape, f32),
        in_specs=[pl.BlockSpec(memory_space=pltpu.SMEM)] + [anywhere] * 5,
        out_specs=pl.BlockSpec(memory_space=pltpu.VMEM),
        scratch_shapes=[
            pltpu.VMEM((4, cx + 2, cy, cz), f32),
            pltpu.VMEM((3, cx + 2, cy, cz), f32),
            pltpu.VMEM((cx + 2, cy, cz), f32),
            pltpu.VMEM((4, cx + 2, cy, cz), f32),
            pltpu.VMEM((cx, cy, cz), jnp.int32),
            pltpu.VMEM((7, cx, cy, cz), f32),
            pltpu.VMEM((2, 4, cx, 1, cz), f32),
            pltpu.VMEM((2, 3, cx, 1, cz), f32),
            pltpu.VMEM((2, cx, 1, cz), f32),
            pltpu.VMEM((2, 4, cx, 1, cz), f32),
            pltpu.VMEM((2, cx, 1, cz), f32),
            pltpu.VMEM((2, 4, cx, 1, cz), f32),
            pltpu.VMEM((3, cx, cy, cz), f32),
            pltpu.VMEM((3, cx, cy, cz), f32),
            pltpu.VMEM((cx, cz), f32),
            pltpu.SemaphoreType.DMA((3,)),
            pltpu.SemaphoreType.DMA((18,)),
            pltpu.SemaphoreType.DMA((18,)),
        ],
        compiler_params=pltpu.CompilerParams(
            collective_id=0, has_side_effects=True, vmem_limit_bytes=60 * 1024 * 1024
        ),
        name="adjoint_steps",
    )(
        fringe_range,
        wind,
        wind.reshape(3, cx, cy, 1, cz),
        adjoint,
        adjoint.reshape(4, cx, cy, 1, cz),
        turbines,
    )


def solution(mesh):
    in_specs = (
        P("dom", None, "gx", "gy", None),
        P("dom", None, "gx", "gy", None),
        P("gx", "gy", None),
        P(),
    )
    out_specs = P("dom", None, "gx", "gy", None)
    return jax.shard_map(
        on_device, mesh=mesh, in_specs=in_specs, out_specs=out_specs, check_vma=False
    )
```

```python
import functools
import math

import jax
import jax.numpy as jnp
from jax import lax
from jax.experimental import pallas as pl
from jax.experimental.pallas import tpu as pltpu
from jax.sharding import PartitionSpec as P

DT = 0.1
SMAG = 0.1
SOUND_SQ = 4.0
DRAG = 1.0
RATE = 3.0
H = 0.5 * DT
GROUP = 7


def shifted_z(field):
    depth = field.shape[-1]
    lane = lax.broadcasted_iota(jnp.int32, field.shape, 1)
    after = jnp.where(lane == depth - 1, 0.0, pltpu.roll(field, depth - 1, 1))
    before = jnp.where(lane == 0, 0.0, pltpu.roll(field, 1, 1))
    return after, before


def shifted_y(field, row_after, row_before):
    rows = field.shape[0]
    row = lax.broadcasted_iota(jnp.int32, field.shape, 0)
    after = jnp.where(row == rows - 1, row_after, pltpu.roll(field, rows - 1, 0))
    before = jnp.where(row == 0, row_before, pltpu.roll(field, 1, 0))
    return after, before


def neighbours(ext, c, x, rows=None, lower=True, upper=True):
    here = ext[c, x + 1]
    nothing = jnp.zeros_like(here)
    after, before = (0.0, 0.0) if rows is None else (rows[1, c, x], rows[0, c, x])
    yp, ym = shifted_y(here, after, before)
    zp, zm = shifted_z(here)
    xp = ext[c, x + 2] if upper else nothing
    xm = ext[c, x] if lower else nothing
    return here, xp, xm, yp, ym, zp, zm


def kernel(
    sizes,
    fringe,
    wind,
    adjoint,
    turbines,
    out,
    a_ext,
    w_ext,
    n_ext,
    b_ext,
    turb,
    coef,
    a_in,
    w_in,
    n_in,
    b_in,
    a_out,
    w_out,
    n_out,
    b_out,
    first_main,
    second_main,
    rates,
    load_sem,
    send_sem,
    recv_sem,
):
    n_gx, n_gy = sizes
    cells_x, cells_y, cells_z = turb.shape
    dom, gx, gy = (lax.axis_index(a) for a in ("dom", "gx", "gy"))
    total = cells_x * n_gx
    reach = total // 4 - 1
    is_main = dom == 0
    in_fringe = jnp.logical_or(gx == n_gx - 1, gx * cells_x < reach)
    sends_forcing = jnp.logical_and(is_main, in_fringe)
    gets_forcing = jnp.logical_and(jnp.logical_not(is_main), in_fringe)
    up_x, down_x = lax.rem(gx + 1, n_gx), lax.rem(gx + n_gx - 1, n_gx)
    up_y, down_y = lax.rem(gy + 1, n_gy), lax.rem(gy + n_gy - 1, n_gy)
    places = ({"gx": up_x}, {"gx": down_x}, {"gy": up_y}, {"gy": down_y})
    partner = {"dom": 1 - dom}

    def remote(src, dst, slot, device):
        return pltpu.make_async_remote_copy(
            src_ref=src,
            dst_ref=dst,
            send_sem=send_sem.at[slot],
            recv_sem=recv_sem.at[slot],
            device_id=device,
            device_id_type=pl.DeviceIdType.MESH,
        )

    load_wind = pltpu.make_async_copy(wind.at[0], w_ext.at[:, pl.ds(1, cells_x)], load_sem.at[0])
    load_adjoint = pltpu.make_async_copy(
        adjoint.at[0], a_ext.at[:, pl.ds(1, cells_x)], load_sem.at[1]
    )
    load_turbines = pltpu.make_async_copy(turbines, turb, load_sem.at[2])
    load_wind.start()

    barrier = pltpu.get_barrier_semaphore()
    for place in places + (partner,):
        pl.semaphore_signal(
            barrier, inc=1, device_id=place, device_id_type=pl.DeviceIdType.MESH
        )
    load_adjoint.start()
    load_turbines.start()

    position = gx * cells_x + lax.broadcasted_iota(jnp.int32, (cells_x, cells_z), 0)
    offset = position - fringe[0]
    offset = jnp.where(offset < 0, offset + total, offset)
    phase = math.pi * (offset.astype(jnp.float32) + 0.5) / fringe[1].astype(jnp.float32)
    sine = jnp.sin(phase)
    sign = jnp.where(is_main, -DT, DT)
    rates[...] = jnp.where(offset < fringe[1], sign * (RATE * sine * sine), 0.0)

    def for_slabs(body):
        body(0, lower=False)
        body(cells_x - 1, upper=False)
        inner = cells_x - 2
        size = max(g for g in range(1, GROUP + 1) if inner % g == 0)

        def several(i, carry):
            for k in range(size):
                body(1 + i * size + k)
            return carry

        lax.fori_loop(0, inner // size, several, 0)

    first_row, last_row = pl.ds(0, 1), pl.ds(cells_y - 1, 1)

    def pack(ext, packed, comps):
        def body(x, **_):
            for c in range(comps):
                packed[0, c, x] = ext[c, x + 1, last_row]
                packed[1, c, x] = ext[c, x + 1, first_row]

        for_slabs(body)

    load_wind.wait()
    pack(w_ext, w_out, 3)
    load_adjoint.wait()
    pack(a_ext, a_out, 4)
    pl.semaphore_wait(barrier, len(places) + 1)

    def exchange(slot, ext, packed, sides):
        pieces = (
            remote(ext.at[:, cells_x], ext.at[:, 0], slot, places[0]),
            remote(ext.at[:, 1], ext.at[:, cells_x + 1], slot + 1, places[1]),
            remote(packed.at[0], sides.at[0], slot + 2, places[2]),
            remote(packed.at[1], sides.at[1], slot + 3, places[3]),
        )
        for k in (2, 3, 0, 1):
            pieces[k].start()
        return pieces

    wind_copies = exchange(0, w_ext, w_out, w_in)
    adjoint_copies = exchange(4, a_ext, a_out, a_in)
    inside = pl.ds(1, cells_x)
    first_forcing = remote(a_ext.at[pl.ds(0, 3), inside], first_main, 16, partner)

    @pl.when(sends_forcing)
    def _():
        first_forcing.start()

    for piece in wind_copies:
        piece.wait_recv()

    def viscosity(x, **_):
        grads = []
        for c in range(3):
            _, xp, xm, yp, ym, zp, zm = neighbours(w_ext, c, x, w_in)
            grads.append((xp - xm, yp - ym, zp - zm))
        own = sum(grads[k][k] * grads[k][k] for k in range(3))
        xy = grads[0][1] + grads[1][0]
        xz = grads[0][2] + grads[2][0]
        yz = grads[1][2] + grads[2][1]
        nu = (0.5 * SMAG) * jnp.sqrt(2.0 * own + (xy * xy + xz * xz + yz * yz))
        n_ext[0, x + 1] = nu
        n_out[0, 0, x] = nu[cells_y - 1 :]
        n_out[1, 0, x] = nu[:1]

    for_slabs(viscosity)
    viscosity_copies = exchange(8, n_ext, n_out, n_in)

    load_turbines.wait()
    for piece in adjoint_copies:
        piece.wait_recv()

    drag_scale = jnp.where(is_main, DT * DRAG, 0.0)
    own_scale = jnp.where(is_main, 1.0, 0.0)

    def coefficients(x, **edges):
        u, v, w = w_ext[0, x + 1], w_ext[1, x + 1], w_ext[2, x + 1]
        nu, *faces = neighbours(n_ext, 0, x, **edges)
        nxp, nxm, nyp, nym, nzp, nzm = (face + nu for face in faces)
        speed = jnp.sqrt(u * u + v * v + w * w)
        drag = drag_scale * turb[x].astype(jnp.float32) * speed
        around = (nxp + nxm) + (nyp + nym) + (nzp + nzm)
        forcing = own_scale * rates[pl.ds(x, 1)]
        return (
            (1.0 + forcing) - H * around - drag,
            H * (nxp + u),
            H * (nxm - u),
            H * (nyp + v),
            H * (nym - v),
            H * (nzp + w),
            H * (nzm - w),
        )

    def advance(ext, weights, x, **edges):
        u, v, w = w_ext[0, x + 1], w_ext[1, x + 1], w_ext[2, x + 1]
        p, pxp, pxm, pyp, pym, pzp, pzm = neighbours(ext, 3, x, **edges)
        slopes = (pxp - pxm, pyp - pym, pzp - pzm)
        gain = u * slopes[0] + v * slopes[1] + w * slopes[2]
        results = []
        for c in range(3):
            stencil = neighbours(ext, c, x, **edges)
            gain = gain + (stencil[1 + 2 * c] - stencil[2 + 2 * c])
            new = sum(k * f for k, f in zip(weights, stencil))
            results.append(new + (SOUND_SQ * H) * slopes[c])
        results.append(p + H * gain)
        return results

    def first_step(x, **edges):
        weights = coefficients(x, **edges)
        for k, weight in enumerate(weights):
            coef[k, x] = weight
        for c, new in enumerate(advance(a_ext, weights, x, rows=a_in)):
            b_ext[c, x + 1] = new
        b_out[0, 3, x] = new[cells_y - 1 :]
        b_out[1, 3, x] = new[:1]

    for_slabs(first_step)

    @pl.when(gets_forcing)
    def _():
        first_forcing.wait_recv()

        def add(x, **_):
            rate = rates[pl.ds(x, 1)]
            for c in range(3):
                b_ext[c, x + 1] += rate * first_main[c, x]

        for_slabs(add)

    for piece in viscosity_copies:
        piece.wait_recv()
    ends = ((0, 0, 2), (cells_x - 1, cells_x + 1, 1))
    edges_y = ((0, first_row, 4), (1, last_row, 3))
    for x, halo, _ in ends:
        nu = H * n_ext[0, halo]
        for c in range(3):
            b_ext[c, x + 1] += nu * (a_ext[c, halo] - a_ext[c, x + 1])

    def first_rows(x, **_):
        for side, row, _ in edges_y:
            nu = H * n_in[side, 0, x]
            for c in range(3):
                change = nu * (a_in[side, c, x] - a_ext[c, x + 1, row])
                new = b_ext[c, x + 1, row] + change
                b_ext[c, x + 1, row] = new
                b_out[1 - side, c, x] = new

    for_slabs(first_rows)
    second_copies = exchange(12, b_ext, b_out, b_in)
    second_forcing = remote(b_ext.at[pl.ds(0, 3), inside], second_main, 17, partner)

    @pl.when(sends_forcing)
    def _():
        second_forcing.start()

    for x, halo, k in ends:
        nu = H * n_ext[0, halo]
        coef[0, x] -= nu
        coef[k, x] += nu

    def coefficient_rows(x, **_):
        for side, row, k in edges_y:
            nu = H * n_in[side, 0, x]
            coef[0, x, row] -= nu
            coef[k, x, row] += nu

    for_slabs(coefficient_rows)

    def second_step(x, **edges):
        weights = tuple(coef[k, x] for k in range(7))
        for c, new in enumerate(advance(b_ext, weights, x, **edges)):
            out[0, c, x] = new

    for_slabs(second_step)

    for piece in second_copies:
        piece.wait_recv()

    def halo_terms(weight, velocity, layer, along, sign):
        terms = [weight * layer[c] for c in range(3)]
        terms[along] = terms[along] + (sign * SOUND_SQ * H) * layer[3]
        terms.append((sign * H) * (velocity * layer[3] + layer[along]))
        return terms

    for x, halo, k in ends:
        layer = [b_ext[c, halo] for c in range(4)]
        sign = -1.0 if k == 2 else 1.0
        for c, term in enumerate(halo_terms(coef[k, x], w_ext[0, x + 1], layer, 0, sign)):
            out[0, c, x] += term

    def second_rows(x, **_):
        for side, row, k in edges_y:
            layer = [b_in[side, c, x] for c in range(4)]
            sign = -1.0 if side == 0 else 1.0
            terms = halo_terms(coef[k, x, row], w_ext[1, x + 1, row], layer, 1, sign)
            for c, term in enumerate(terms):
                out[0, c, x, row] += term

    for_slabs(second_rows)

    @pl.when(gets_forcing)
    def _():
        second_forcing.wait_recv()

        def add(x, **_):
            rate = rates[pl.ds(x, 1)]
            for c in range(3):
                out[0, c, x] += rate * second_main[c, x]

        for_slabs(add)

    for piece in wind_copies + adjoint_copies + viscosity_copies + second_copies:
        piece.wait_send()

    @pl.when(sends_forcing)
    def _():
        first_forcing.wait_send()
        second_forcing.wait_send()


def on_device(wind, adjoint, turbines, fringe_range):
    _, _, cx, cy, cz = wind.shape
    f32 = jnp.float32
    sizes = (lax.axis_size("gx"), lax.axis_size("gy"))
    anywhere = pl.BlockSpec(memory_space=pltpu.HBM)
    return pl.pallas_call(
        functools.partial(kernel, sizes),
        out_shape=pltpu.VMEM(adjoint.shape, f32),
        in_specs=[pl.BlockSpec(memory_space=pltpu.SMEM)] + [anywhere] * 3,
        out_specs=pl.BlockSpec(memory_space=pltpu.VMEM),
        scratch_shapes=[
            pltpu.VMEM((4, cx + 2, cy, cz), f32),
            pltpu.VMEM((3, cx + 2, cy, cz), f32),
            pltpu.VMEM((1, cx + 2, cy, cz), f32),
            pltpu.VMEM((4, cx + 2, cy, cz), f32),
            pltpu.VMEM((cx, cy, cz), jnp.int32),
            pltpu.VMEM((7, cx, cy, cz), f32),
            pltpu.VMEM((2, 4, cx, 1, cz), f32),
            pltpu.VMEM((2, 3, cx, 1, cz), f32),
            pltpu.VMEM((2, 1, cx, 1, cz), f32),
            pltpu.VMEM((2, 4, cx, 1, cz), f32),
            pltpu.VMEM((2, 4, cx, 1, cz), f32),
            pltpu.VMEM((2, 3, cx, 1, cz), f32),
            pltpu.VMEM((2, 1, cx, 1, cz), f32),
            pltpu.VMEM((2, 4, cx, 1, cz), f32),
            pltpu.VMEM((3, cx, cy, cz), f32),
            pltpu.VMEM((3, cx, cy, cz), f32),
            pltpu.VMEM((cx, cz), f32),
            pltpu.SemaphoreType.DMA((3,)),
            pltpu.SemaphoreType.DMA((18,)),
            pltpu.SemaphoreType.DMA((18,)),
        ],
        compiler_params=pltpu.CompilerParams(
            collective_id=0, has_side_effects=True, vmem_limit_bytes=60 * 1024 * 1024
        ),
        name="adjoint_steps",
    )(
        fringe_range,
        wind,
        adjoint,
        turbines,
    )


def solution(mesh):
    in_specs = (
        P("dom", None, "gx", "gy", None),
        P("dom", None, "gx", "gy", None),
        P("gx", "gy", None),
        P(),
    )
    out_specs = P("dom", None, "gx", "gy", None)
    return jax.shard_map(
        on_device, mesh=mesh, in_specs=in_specs, out_specs=out_specs, check_vma=False
    )
```

```python
import functools
import math

import jax
import jax.numpy as jnp
from jax import lax
from jax.experimental import pallas as pl
from jax.experimental.pallas import tpu as pltpu
from jax.sharding import PartitionSpec as P

DT = 0.1
SMAG = 0.1
SOUND_SQ = 4.0
DRAG = 1.0
RATE = 3.0
H = 0.5 * DT
GROUP = 7


def shifted_z(field):
    depth = field.shape[-1]
    lane = lax.broadcasted_iota(jnp.int32, field.shape, 1)
    after = jnp.where(lane == depth - 1, 0.0, pltpu.roll(field, depth - 1, 1))
    before = jnp.where(lane == 0, 0.0, pltpu.roll(field, 1, 1))
    return after, before


def shifted_y(field):
    rows = field.shape[0]
    row = lax.broadcasted_iota(jnp.int32, field.shape, 0)
    after = jnp.where(row == rows - 1, 0.0, pltpu.roll(field, rows - 1, 0))
    before = jnp.where(row == 0, 0.0, pltpu.roll(field, 1, 0))
    return after, before


def kernel(
    sizes,
    fringe_hbm,
    wind,
    adjoint,
    turbines,
    out,
    a_ext,
    w_ext,
    n_ext,
    b_ext,
    turb,
    coef,
    a_in,
    w_in,
    n_in,
    b_in,
    a_out,
    w_out,
    n_out,
    b_out,
    first_main,
    second_main,
    rates,
    fringe,
    load_sem,
    send_sem,
    recv_sem,
):
    n_gx, n_gy, cells_x, cells_y = sizes
    cells_z = turb.shape[-1]
    dom, gx, gy = (lax.axis_index(a) for a in ("dom", "gx", "gy"))
    total = cells_x * n_gx
    reach = total // 4 - 1
    is_main = dom == 0
    in_fringe = jnp.logical_or(gx == n_gx - 1, gx * cells_x < reach)
    sends_forcing = jnp.logical_and(is_main, in_fringe)
    gets_forcing = jnp.logical_and(jnp.logical_not(is_main), in_fringe)
    up_x, down_x = lax.rem(gx + 1, n_gx), lax.rem(gx + n_gx - 1, n_gx)
    up_y, down_y = lax.rem(gy + 1, n_gy), lax.rem(gy + n_gy - 1, n_gy)
    places = ({"gx": up_x}, {"gx": down_x}, {"gy": up_y}, {"gy": down_y})
    partner = {"dom": 1 - dom}

    def remote(src, dst, slot, device):
        return pltpu.make_async_remote_copy(
            src_ref=src,
            dst_ref=dst,
            send_sem=send_sem.at[slot],
            recv_sem=recv_sem.at[slot],
            device_id=device,
            device_id_type=pl.DeviceIdType.MESH,
        )

    inside = pl.ds(cells_y, cells_x * cells_y)
    load_fringe = pltpu.make_async_copy(fringe_hbm, fringe, load_sem.at[3])
    load_wind = pltpu.make_async_copy(wind, w_ext.at[:, inside], load_sem.at[0])
    load_adjoint = pltpu.make_async_copy(adjoint, a_ext.at[:, inside], load_sem.at[1])
    load_turbines = pltpu.make_async_copy(turbines, turb, load_sem.at[2])

    barrier = pltpu.get_barrier_semaphore()
    for place in places + (partner,):
        pl.semaphore_signal(
            barrier, inc=1, device_id=place, device_id_type=pl.DeviceIdType.MESH
        )
    load_wind.start()
    load_fringe.start()
    load_adjoint.start()
    load_turbines.start()
    pl.semaphore_wait(barrier, len(places) + 1)

    def slab(x):
        return pl.ds(pl.multiple_of(x * cells_y, 8), cells_y)

    def row(y, shift=0):
        return pl.ds(shift * cells_y + y, cells_x, stride=cells_y)

    def copies_x(slot, ext, last, first):
        pieces = (
            remote(last, ext.at[:, slab(0)], slot, places[0]),
            remote(first, ext.at[:, slab(cells_x + 1)], slot + 1, places[1]),
        )
        for piece in pieces:
            piece.start()
        return pieces

    def copies_y(slot, packed, sides):
        pieces = (
            remote(packed.at[0], sides.at[0], slot + 2, places[2]),
            remote(packed.at[1], sides.at[1], slot + 3, places[3]),
        )
        for piece in pieces:
            piece.start()
        return pieces

    def pack(ext, packed, comps):
        for c in range(comps):
            packed[0, c] = ext[c, row(cells_y - 1, 1)]
            packed[1, c] = ext[c, row(0, 1)]

    wind_copies = copies_x(0, w_ext, wind.at[:, slab(cells_x - 1)], wind.at[:, slab(0)])
    adjoint_copies = copies_x(
        4, a_ext, adjoint.at[:, slab(cells_x - 1)], adjoint.at[:, slab(0)]
    )
    load_wind.wait()
    pack(w_ext, w_out, 3)
    wind_copies += copies_y(0, w_out, w_in)
    load_adjoint.wait()
    pack(a_ext, a_out, 4)
    adjoint_copies += copies_y(4, a_out, a_in)
    first_forcing = remote(a_ext.at[pl.ds(0, 3), inside], first_main, 16, partner)

    @pl.when(sends_forcing)
    def _():
        first_forcing.start()

    def for_inner(body):
        inner = cells_x - 2
        size = max(g for g in range(1, GROUP + 1) if inner % g == 0)

        def several(i, carry):
            for k in range(size):
                body(1 + i * size + k)
            return carry

        lax.fori_loop(0, inner // size, several, 0)

    def for_slabs(body):
        body(0, lower=False)
        body(cells_x - 1, upper=False)
        for_inner(body)

    def neighbours(ext, c, x, lower=True, upper=True):
        here = ext[c, slab(x + 1)]
        nothing = jnp.zeros_like(here)
        xp = ext[c, slab(x + 2)] if upper else nothing
        xm = ext[c, slab(x)] if lower else nothing
        return (here, xp, xm, *shifted_y(here), *shifted_z(here))

    def strain(stencils):
        grads = []
        for _, xp, xm, yp, ym, zp, zm in stencils:
            grads.append((xp - xm, yp - ym, zp - zm))
        own = sum(grads[k][k] * grads[k][k] for k in range(3))
        xy = grads[0][1] + grads[1][0]
        xz = grads[0][2] + grads[2][0]
        yz = grads[1][2] + grads[2][1]
        return (0.5 * SMAG) * jnp.sqrt(2.0 * own + (xy * xy + xz * xz + yz * yz))

    def viscosity(x):
        n_ext[0, slab(x + 1)] = strain([neighbours(w_ext, c, x) for c in range(3)])

    for_inner(viscosity)
    for piece in wind_copies:
        piece.wait_recv()
    viscosity(0)
    viscosity(cells_x - 1)
    for side, y, inward in ((0, 0, 1), (1, cells_y - 1, cells_y - 2)):
        stencils = []
        for c in range(3):
            here, halo, near = w_ext[c, row(y, 1)], w_in[side, c], w_ext[c, row(inward, 1)]
            along_y = (near, halo) if side == 0 else (halo, near)
            along_x = (w_ext[c, row(y, 2)], w_ext[c, row(y, 0)])
            stencils.append((here, *along_x, *along_y, *shifted_z(here)))
        nu = strain(stencils)
        n_out[1 - side, 0] = nu
        n_ext[0, row(y, 1)] = nu
    viscosity_copies = copies_y(8, n_out, n_in)
    viscosity_copies += copies_x(8, n_ext, n_ext.at[:, slab(cells_x)], n_ext.at[:, slab(1)])

    load_fringe.wait()
    position = gx * cells_x + lax.broadcasted_iota(jnp.int32, (cells_x, cells_z), 0)
    offset = position - fringe[0]
    offset = jnp.where(offset < 0, offset + total, offset)
    phase = math.pi * (offset.astype(jnp.float32) + 0.5) / fringe[1].astype(jnp.float32)
    sine = jnp.sin(phase)
    sign = jnp.where(is_main, -DT, DT)
    rates[...] = jnp.where(offset < fringe[1], sign * (RATE * sine * sine), 0.0)

    load_turbines.wait()
    drag_scale = jnp.where(is_main, DT * DRAG, 0.0)
    own_scale = jnp.where(is_main, 1.0, 0.0)

    def coefficients(x, **edges):
        u, v, w = (w_ext[c, slab(x + 1)] for c in range(3))
        nu, *faces = neighbours(n_ext, 0, x, **edges)
        nxp, nxm, nyp, nym, nzp, nzm = (face + nu for face in faces)
        speed = jnp.sqrt(u * u + v * v + w * w)
        drag = drag_scale * turb[slab(x)].astype(jnp.float32) * speed
        around = (nxp + nxm) + (nyp + nym) + (nzp + nzm)
        forcing = own_scale * rates[pl.ds(x, 1)]
        return (
            (1.0 + forcing) - H * around - drag,
            H * (nxp + u),
            H * (nxm - u),
            H * (nyp + v),
            H * (nym - v),
            H * (nzp + w),
            H * (nzm - w),
        )

    def advance(ext, weights, x, **edges):
        u, v, w = (w_ext[c, slab(x + 1)] for c in range(3))
        p, pxp, pxm, pyp, pym, pzp, pzm = neighbours(ext, 3, x, **edges)
        slopes = (pxp - pxm, pyp - pym, pzp - pzm)
        gain = u * slopes[0] + v * slopes[1] + w * slopes[2]
        results = []
        for c in range(3):
            stencil = neighbours(ext, c, x, **edges)
            gain = gain + (stencil[1 + 2 * c] - stencil[2 + 2 * c])
            new = sum(k * f for k, f in zip(weights, stencil))
            results.append(new + (SOUND_SQ * H) * slopes[c])
        results.append(p + H * gain)
        return results

    def first_step(x, **edges):
        weights = coefficients(x, **edges)
        for k, weight in enumerate(weights):
            coef[k, slab(x)] = weight
        for c, new in enumerate(advance(a_ext, weights, x, **edges)):
            b_ext[c, slab(x + 1)] = new

    for_slabs(first_step)

    @pl.when(gets_forcing)
    def _():
        first_forcing.wait_recv()

        def add(x, **_):
            rate = rates[pl.ds(x, 1)]
            for c in range(3):
                b_ext[c, slab(x + 1)] += rate * first_main[c, slab(x)]

        for_slabs(add)

    def of_side(side):
        return lambda ext, sides, c: sides[side, c]

    def of_slab(x):
        return lambda ext, sides, c: ext[c, slab(x)]

    layers = (
        (slab(0), slab(1), of_slab(0), 2, 0, -1.0),
        (slab(cells_x - 1), slab(cells_x), of_slab(cells_x + 1), 1, 0, 1.0),
        (row(0), row(0, 1), of_side(0), 4, 1, -1.0),
        (row(cells_y - 1), row(cells_y - 1, 1), of_side(1), 3, 1, 1.0),
    )

    def halo_terms(weight, velocity, layer, along, sign):
        terms = [weight * layer[c] for c in range(3)]
        terms[along] = terms[along] + (sign * SOUND_SQ * H) * layer[3]
        terms.append((sign * H) * (velocity * layer[3] + layer[along]))
        return terms

    for piece in adjoint_copies + viscosity_copies:
        piece.wait_recv()
    for place, extended, layer_of, k, along, sign in layers:
        nu = H * layer_of(n_ext, n_in, 0)
        weight = coef[k, place] + nu
        coef[k, place] = weight
        coef[0, place] -= nu
        layer = [layer_of(a_ext, a_in, c) for c in range(4)]
        terms = halo_terms(weight, w_ext[along, extended], layer, along, sign)
        for c in range(4):
            new = b_ext[c, extended] + terms[c]
            if c < 3:
                new = new - nu * a_ext[c, extended]
            b_ext[c, extended] = new
            if along == 1:
                b_out[1 if sign < 0 else 0, c] = new
    second_copies = copies_y(12, b_out, b_in)
    second_copies += copies_x(12, b_ext, b_ext.at[:, slab(cells_x)], b_ext.at[:, slab(1)])
    second_forcing = remote(b_ext.at[pl.ds(0, 3), inside], second_main, 17, partner)

    @pl.when(sends_forcing)
    def _():
        second_forcing.start()

    def second_step(x, **edges):
        weights = tuple(coef[k, slab(x)] for k in range(7))
        for c, new in enumerate(advance(b_ext, weights, x, **edges)):
            out[c, slab(x)] = new

    for_slabs(second_step)

    for piece in second_copies:
        piece.wait_recv()
    for place, extended, layer_of, k, along, sign in layers:
        layer = [layer_of(b_ext, b_in, c) for c in range(4)]
        terms = halo_terms(coef[k, place], w_ext[along, extended], layer, along, sign)
        for c in range(4):
            out[c, place] += terms[c]

    @pl.when(gets_forcing)
    def _():
        second_forcing.wait_recv()

        def add(x, **_):
            rate = rates[pl.ds(x, 1)]
            for c in range(3):
                out[c, slab(x)] += rate * second_main[c, slab(x)]

        for_slabs(add)

    for piece in wind_copies + adjoint_copies + viscosity_copies + second_copies:
        piece.wait_send()

    @pl.when(sends_forcing)
    def _():
        first_forcing.wait_send()
        second_forcing.wait_send()


def on_device(wind, adjoint, turbines, fringe_range):
    _, _, cx, cy, cz = wind.shape
    f32 = jnp.float32
    sizes = (lax.axis_size("gx"), lax.axis_size("gy"), cx, cy)
    around, tile = (cx + 2) * cy, cx * cy
    later = pl.pallas_call(
        functools.partial(kernel, sizes),
        out_shape=pltpu.VMEM((4, tile, cz), f32),
        in_specs=[pl.BlockSpec(memory_space=pltpu.HBM)] * 4,
        out_specs=pl.BlockSpec(memory_space=pltpu.VMEM),
        scratch_shapes=[
            pltpu.VMEM((4, around, cz), f32),
            pltpu.VMEM((3, around, cz), f32),
            pltpu.VMEM((1, around, cz), f32),
            pltpu.VMEM((4, around, cz), f32),
            pltpu.VMEM((tile, cz), jnp.int32),
            pltpu.VMEM((7, tile, cz), f32),
            pltpu.VMEM((2, 4, cx, cz), f32),
            pltpu.VMEM((2, 3, cx, cz), f32),
            pltpu.VMEM((2, 1, cx, cz), f32),
            pltpu.VMEM((2, 4, cx, cz), f32),
            pltpu.VMEM((2, 4, cx, cz), f32),
            pltpu.VMEM((2, 3, cx, cz), f32),
            pltpu.VMEM((2, 1, cx, cz), f32),
            pltpu.VMEM((2, 4, cx, cz), f32),
            pltpu.VMEM((3, tile, cz), f32),
            pltpu.VMEM((3, tile, cz), f32),
            pltpu.VMEM((cx, cz), f32),
            pltpu.SMEM((2,), jnp.int32),
            pltpu.SemaphoreType.DMA((4,)),
            pltpu.SemaphoreType.DMA((18,)),
            pltpu.SemaphoreType.DMA((18,)),
        ],
        compiler_params=pltpu.CompilerParams(
            collective_id=0, has_side_effects=True, vmem_limit_bytes=60 * 1024 * 1024
        ),
        name="adjoint_steps",
    )(
        fringe_range,
        wind.reshape(3, tile, cz),
        adjoint.reshape(4, tile, cz),
        turbines.reshape(tile, cz),
    )
    return later.reshape(adjoint.shape)


def solution(mesh):
    in_specs = (
        P("dom", None, "gx", "gy", None),
        P("dom", None, "gx", "gy", None),
        P("gx", "gy", None),
        P(),
    )
    out_specs = P("dom", None, "gx", "gy", None)
    return jax.shard_map(
        on_device, mesh=mesh, in_specs=in_specs, out_specs=out_specs, check_vma=False
    )
```

```python
import functools
import math

import jax
import jax.numpy as jnp
from jax import lax
from jax.experimental import pallas as pl
from jax.experimental.pallas import tpu as pltpu
from jax.sharding import PartitionSpec as P

DT = 0.1
SMAG = 0.1
SOUND_SQ = 4.0
DRAG = 1.0
RATE = 3.0
H = 0.5 * DT
GROUP = 7


def shifted_z(field):
    depth = field.shape[-1]
    lane = lax.broadcasted_iota(jnp.int32, field.shape, 1)
    after = jnp.where(lane == depth - 1, 0.0, pltpu.roll(field, depth - 1, 1))
    before = jnp.where(lane == 0, 0.0, pltpu.roll(field, 1, 1))
    return after, before


def shifted_y(field, row_after=0.0, row_before=0.0):
    rows = field.shape[0]
    row = lax.broadcasted_iota(jnp.int32, field.shape, 0)
    after = jnp.where(row == rows - 1, row_after, pltpu.roll(field, rows - 1, 0))
    before = jnp.where(row == 0, row_before, pltpu.roll(field, 1, 0))
    return after, before


def kernel(
    sizes,
    fringe_hbm,
    wind,
    adjoint,
    turbines,
    out,
    a_ext,
    w_ext,
    n_ext,
    b_ext,
    turb,
    coef,
    a_in,
    w_in,
    n_in,
    b_in,
    a_out,
    w_out,
    b_out,
    corner_in,
    corner_out,
    w_row,
    first_main,
    second_main,
    rates,
    fringe,
    load_sem,
    send_sem,
    recv_sem,
):
    n_gx, n_gy, cells_x, cells_y = sizes
    cells_z = turb.shape[-1]
    dom, gx, gy = (lax.axis_index(a) for a in ("dom", "gx", "gy"))
    total = cells_x * n_gx
    reach = total // 4 - 1
    is_main = dom == 0
    in_fringe = jnp.logical_or(gx == n_gx - 1, gx * cells_x < reach)
    sends_forcing = jnp.logical_and(is_main, in_fringe)
    gets_forcing = jnp.logical_and(jnp.logical_not(is_main), in_fringe)
    up_x, down_x = lax.rem(gx + 1, n_gx), lax.rem(gx + n_gx - 1, n_gx)
    up_y, down_y = lax.rem(gy + 1, n_gy), lax.rem(gy + n_gy - 1, n_gy)
    places = ({"gx": up_x}, {"gx": down_x}, {"gy": up_y}, {"gy": down_y})
    partner = {"dom": 1 - dom}
    diagonal = tuple({"gx": x, "gy": y} for x in (up_x, down_x) for y in (up_y, down_y))

    def remote(src, dst, slot, device):
        return pltpu.make_async_remote_copy(
            src_ref=src,
            dst_ref=dst,
            send_sem=send_sem.at[slot],
            recv_sem=recv_sem.at[slot],
            device_id=device,
            device_id_type=pl.DeviceIdType.MESH,
        )

    inside = pl.ds(cells_y, cells_x * cells_y)
    inside_wind = pl.ds(2 * cells_y, cells_x * cells_y)
    load_fringe = pltpu.make_async_copy(fringe_hbm, fringe, load_sem.at[3])
    load_wind = pltpu.make_async_copy(wind, w_ext.at[:, inside_wind], load_sem.at[0])
    load_adjoint = pltpu.make_async_copy(adjoint, a_ext.at[:, inside], load_sem.at[1])
    load_turbines = pltpu.make_async_copy(turbines, turb, load_sem.at[2])

    barrier = pltpu.get_barrier_semaphore()
    for place in places + diagonal + (partner,):
        pl.semaphore_signal(
            barrier, inc=1, device_id=place, device_id_type=pl.DeviceIdType.MESH
        )
    load_wind.start()
    load_fringe.start()
    load_adjoint.start()
    load_turbines.start()
    pl.semaphore_wait(barrier, len(places) + len(diagonal) + 1)

    def slab(x):
        return pl.ds(pl.multiple_of(x * cells_y, 8), cells_y)

    def row(y, shift=0):
        return pl.ds(shift * cells_y + y, cells_x, stride=cells_y)

    def copies_x(slot, ext, last, first, depth):
        span = depth * cells_y
        pieces = (
            remote(last, ext.at[:, pl.ds(0, span)], slot, places[0]),
            remote(first, ext.at[:, pl.ds(cells_x * cells_y + span, span)], slot + 1, places[1]),
        )
        for piece in pieces:
            piece.start()
        return pieces

    def copies_y(slot, packed, sides):
        pieces = (
            remote(packed.at[0], sides.at[0], slot + 2, places[2]),
            remote(packed.at[1], sides.at[1], slot + 3, places[3]),
        )
        for piece in pieces:
            piece.start()
        return pieces

    span = 2 * cells_y
    wind_copies = copies_x(
        0,
        w_ext,
        wind.at[:, pl.ds((cells_x - 2) * cells_y, span)],
        wind.at[:, pl.ds(0, span)],
        2,
    )
    adjoint_copies = copies_x(
        4, a_ext, adjoint.at[:, slab(cells_x - 1)], adjoint.at[:, slab(0)], 1
    )
    load_wind.wait()
    for c in range(3):
        for j in range(2):
            w_out[0, c, j] = w_ext[c, row(cells_y - 1 - j, 2)]
            w_out[1, c, j] = w_ext[c, row(j, 2)]
    wind_copies += copies_y(0, w_out, w_in)
    corner_copies = []
    for q in range(4):
        x, y = (cells_x - 1, 0)[q // 2], (cells_y - 1, 0)[q % 2]
        for c in range(3):
            corner_out[q, c] = w_ext[c, pl.ds((x + 2) * cells_y + y, 1)]
        piece = remote(corner_out.at[q], corner_in.at[q], 8 + q, diagonal[q])
        piece.start()
        corner_copies.append(piece)
    load_adjoint.wait()
    for c in range(4):
        a_out[0, c] = a_ext[c, row(cells_y - 1, 1)]
        a_out[1, c] = a_ext[c, row(0, 1)]
    adjoint_copies += copies_y(4, a_out, a_in)
    first_forcing = remote(a_ext.at[pl.ds(0, 3), inside], first_main, 16, partner)

    @pl.when(sends_forcing)
    def _():
        first_forcing.start()

    def for_inner(body):
        inner = cells_x - 2
        size = max(g for g in range(1, GROUP + 1) if inner % g == 0)

        def several(i, carry):
            for k in range(size):
                body(1 + i * size + k)
            return carry

        lax.fori_loop(0, inner // size, several, 0)

    def for_slabs(body):
        body(0, lower=False)
        body(cells_x - 1, upper=False)
        for_inner(body)

    def neighbours(ext, c, x, lower=True, upper=True, base=1, rows=(0.0, 0.0)):
        here = ext[c, slab(x + base)]
        nothing = jnp.zeros_like(here)
        xp = ext[c, slab(x + base + 1)] if upper else nothing
        xm = ext[c, slab(x + base - 1)] if lower else nothing
        return (here, xp, xm, *shifted_y(here, *rows), *shifted_z(here))

    def strain(stencils):
        grads = []
        for _, xp, xm, yp, ym, zp, zm in stencils:
            grads.append((xp - xm, yp - ym, zp - zm))
        own = sum(grads[k][k] * grads[k][k] for k in range(3))
        xy = grads[0][1] + grads[1][0]
        xz = grads[0][2] + grads[2][0]
        yz = grads[1][2] + grads[2][1]
        return (0.5 * SMAG) * jnp.sqrt(2.0 * own + (xy * xy + xz * xz + yz * yz))

    def viscosity(x):
        n_ext[0, slab(x + 1)] = strain([neighbours(w_ext, c, x, base=2) for c in range(3)])

    for_inner(viscosity)
    for piece in wind_copies:
        piece.wait_recv()
    viscosity(0)
    viscosity(cells_x - 1)
    for side, y, inward in ((0, 0, 1), (1, cells_y - 1, cells_y - 2)):
        stencils = []
        for c in range(3):
            here, halo, near = w_ext[c, row(y, 2)], w_in[side, c, 0], w_ext[c, row(inward, 2)]
            along_y = (near, halo) if side == 0 else (halo, near)
            along_x = (w_ext[c, row(y, 3)], w_ext[c, row(y, 1)])
            stencils.append((here, *along_x, *along_y, *shifted_z(here)))
        n_ext[0, row(y, 1)] = strain(stencils)

    load_fringe.wait()
    position = gx * cells_x + lax.broadcasted_iota(jnp.int32, (cells_x, cells_z), 0)
    offset = position - fringe[0]
    offset = jnp.where(offset < 0, offset + total, offset)
    phase = math.pi * (offset.astype(jnp.float32) + 0.5) / fringe[1].astype(jnp.float32)
    sine = jnp.sin(phase)
    sign = jnp.where(is_main, -DT, DT)
    rates[...] = jnp.where(offset < fringe[1], sign * (RATE * sine * sine), 0.0)

    load_turbines.wait()
    drag_scale = jnp.where(is_main, DT * DRAG, 0.0)
    own_scale = jnp.where(is_main, 1.0, 0.0)

    def coefficients(x, **edges):
        u, v, w = (w_ext[c, slab(x + 2)] for c in range(3))
        nu, *faces = neighbours(n_ext, 0, x, **edges)
        nxp, nxm, nyp, nym, nzp, nzm = (face + nu for face in faces)
        speed = jnp.sqrt(u * u + v * v + w * w)
        drag = drag_scale * turb[slab(x)].astype(jnp.float32) * speed
        around = (nxp + nxm) + (nyp + nym) + (nzp + nzm)
        forcing = own_scale * rates[pl.ds(x, 1)]
        return (
            (1.0 + forcing) - H * around - drag,
            H * (nxp + u),
            H * (nxm - u),
            H * (nyp + v),
            H * (nym - v),
            H * (nzp + w),
            H * (nzm - w),
        )

    def advance(ext, weights, x, **edges):
        u, v, w = (w_ext[c, slab(x + 2)] for c in range(3))
        p, pxp, pxm, pyp, pym, pzp, pzm = neighbours(ext, 3, x, **edges)
        slopes = (pxp - pxm, pyp - pym, pzp - pzm)
        gain = u * slopes[0] + v * slopes[1] + w * slopes[2]
        results = []
        for c in range(3):
            stencil = neighbours(ext, c, x, **edges)
            gain = gain + (stencil[1 + 2 * c] - stencil[2 + 2 * c])
            new = sum(k * f for k, f in zip(weights, stencil))
            results.append(new + (SOUND_SQ * H) * slopes[c])
        results.append(p + H * gain)
        return results

    def first_step(x, **edges):
        weights = coefficients(x, **edges)
        for k, weight in enumerate(weights):
            coef[k, slab(x)] = weight
        for c, new in enumerate(advance(a_ext, weights, x, **edges)):
            b_ext[c, slab(x + 1)] = new

    for_slabs(first_step)

    @pl.when(gets_forcing)
    def _():
        first_forcing.wait_recv()

        def add(x, **_):
            rate = rates[pl.ds(x, 1)]
            for c in range(3):
                b_ext[c, slab(x + 1)] += rate * first_main[c, slab(x)]

        for_slabs(add)

    def of_side(side):
        return lambda ext, sides, c: sides[side, c]

    def of_slab(x):
        return lambda ext, sides, c: ext[c, slab(x)]

    layers = (
        (slab(0), slab(1), slab(2), of_slab(0), 2, 0, -1.0),
        (slab(cells_x - 1), slab(cells_x), slab(cells_x + 1), of_slab(cells_x + 1), 1, 0, 1.0),
        (row(0), row(0, 1), row(0, 2), of_side(0), 4, 1, -1.0),
        (row(cells_y - 1), row(cells_y - 1, 1), row(cells_y - 1, 2), of_side(1), 3, 1, 1.0),
    )

    def halo_terms(weight, velocity, layer, along, sign):
        terms = [weight * layer[c] for c in range(3)]
        terms[along] = terms[along] + (sign * SOUND_SQ * H) * layer[3]
        terms.append((sign * H) * (velocity * layer[3] + layer[along]))
        return terms

    for piece in corner_copies:
        piece.wait_recv()
    for x, q in ((-1, 0), (cells_x, 2)):
        n_ext[0, slab(x + 1)] = strain(
            [
                neighbours(w_ext, c, x, base=2, rows=(corner_in[q + 1, c], corner_in[q, c]))
                for c in range(3)
            ]
        )
    for side, y in ((0, 0), (1, cells_y - 1)):
        stencils = []
        for c in range(3):
            here, far, near = w_in[side, c, 0], w_in[side, c, 1], w_ext[c, row(y, 2)]
            w_row[side, c, pl.ds(8, cells_x)] = here
            w_row[side, c, pl.ds(7, 1)] = corner_in[side, c]
            w_row[side, c, pl.ds(8 + cells_x, 1)] = corner_in[2 + side, c]
            along_x = (w_row[side, c, pl.ds(9, cells_x)], w_row[side, c, pl.ds(7, cells_x)])
            along_y = (near, far) if side == 0 else (far, near)
            stencils.append((here, *along_x, *along_y, *shifted_z(here)))
        n_in[side, 0] = strain(stencils)

    for piece in adjoint_copies:
        piece.wait_recv()
    for place, extended, windy, layer_of, k, along, sign in layers:
        nu = H * layer_of(n_ext, n_in, 0)
        weight = coef[k, place] + nu
        coef[k, place] = weight
        coef[0, place] -= nu
        layer = [layer_of(a_ext, a_in, c) for c in range(4)]
        terms = halo_terms(weight, w_ext[along, windy], layer, along, sign)
        for c in range(4):
            new = b_ext[c, extended] + terms[c]
            if c < 3:
                new = new - nu * a_ext[c, extended]
            b_ext[c, extended] = new
            if along == 1:
                b_out[1 if sign < 0 else 0, c] = new
    second_copies = copies_y(12, b_out, b_in)
    second_copies += copies_x(12, b_ext, b_ext.at[:, slab(cells_x)], b_ext.at[:, slab(1)], 1)
    second_forcing = remote(b_ext.at[pl.ds(0, 3), inside], second_main, 17, partner)

    @pl.when(sends_forcing)
    def _():
        second_forcing.start()

    def second_step(x, **edges):
        weights = tuple(coef[k, slab(x)] for k in range(7))
        for c, new in enumerate(advance(b_ext, weights, x, **edges)):
            out[c, slab(x)] = new

    for_slabs(second_step)

    for piece in second_copies:
        piece.wait_recv()
    for place, extended, windy, layer_of, k, along, sign in layers:
        layer = [layer_of(b_ext, b_in, c) for c in range(4)]
        terms = halo_terms(coef[k, place], w_ext[along, windy], layer, along, sign)
        for c in range(4):
            out[c, place] += terms[c]

    @pl.when(gets_forcing)
    def _():
        second_forcing.wait_recv()

        def add(x, **_):
            rate = rates[pl.ds(x, 1)]
            for c in range(3):
                out[c, slab(x)] += rate * second_main[c, slab(x)]

        for_slabs(add)

    for piece in (*wind_copies, *corner_copies, *adjoint_copies, *second_copies):
        piece.wait_send()

    @pl.when(sends_forcing)
    def _():
        first_forcing.wait_send()
        second_forcing.wait_send()


def on_device(wind, adjoint, turbines, fringe_range):
    _, _, cx, cy, cz = wind.shape
    f32 = jnp.float32
    sizes = (lax.axis_size("gx"), lax.axis_size("gy"), cx, cy)
    around, tile, wide = (cx + 2) * cy, cx * cy, (cx + 4) * cy
    later = pl.pallas_call(
        functools.partial(kernel, sizes),
        out_shape=pltpu.VMEM((4, tile, cz), f32),
        in_specs=[pl.BlockSpec(memory_space=pltpu.HBM)] * 4,
        out_specs=pl.BlockSpec(memory_space=pltpu.VMEM),
        scratch_shapes=[
            pltpu.VMEM((4, around, cz), f32),
            pltpu.VMEM((3, wide, cz), f32),
            pltpu.VMEM((1, around, cz), f32),
            pltpu.VMEM((4, around, cz), f32),
            pltpu.VMEM((tile, cz), jnp.int32),
            pltpu.VMEM((7, tile, cz), f32),
            pltpu.VMEM((2, 4, cx, cz), f32),
            pltpu.VMEM((2, 3, 2, cx, cz), f32),
            pltpu.VMEM((2, 1, cx, cz), f32),
            pltpu.VMEM((2, 4, cx, cz), f32),
            pltpu.VMEM((2, 4, cx, cz), f32),
            pltpu.VMEM((2, 3, 2, cx, cz), f32),
            pltpu.VMEM((2, 4, cx, cz), f32),
            pltpu.VMEM((4, 3, 1, cz), f32),
            pltpu.VMEM((4, 3, 1, cz), f32),
            pltpu.VMEM((2, 3, cx + 16, cz), f32),
            pltpu.VMEM((3, tile, cz), f32),
            pltpu.VMEM((3, tile, cz), f32),
            pltpu.VMEM((cx, cz), f32),
            pltpu.SMEM((2,), jnp.int32),
            pltpu.SemaphoreType.DMA((4,)),
            pltpu.SemaphoreType.DMA((18,)),
            pltpu.SemaphoreType.DMA((18,)),
        ],
        compiler_params=pltpu.CompilerParams(
            collective_id=0, has_side_effects=True, vmem_limit_bytes=60 * 1024 * 1024
        ),
        name="adjoint_steps",
    )(
        fringe_range,
        wind.reshape(3, tile, cz),
        adjoint.reshape(4, tile, cz),
        turbines.reshape(tile, cz),
    )
    return later.reshape(adjoint.shape)


def solution(mesh):
    in_specs = (
        P("dom", None, "gx", "gy", None),
        P("dom", None, "gx", "gy", None),
        P("gx", "gy", None),
        P(),
    )
    out_specs = P("dom", None, "gx", "gy", None)
    return jax.shard_map(
        on_device, mesh=mesh, in_specs=in_specs, out_specs=out_specs, check_vma=False
    )
```

```python
import functools
import math

import jax
import jax.numpy as jnp
from jax import lax
from jax.experimental import pallas as pl
from jax.experimental.pallas import tpu as pltpu
from jax.sharding import PartitionSpec as P

DT = 0.1
SMAG = 0.1
SOUND_SQ = 4.0
DRAG = 1.0
RATE = 3.0
H = 0.5 * DT
GROUP = 7


def shifted_z(field):
    depth = field.shape[-1]
    lane = lax.broadcasted_iota(jnp.int32, field.shape, 1)
    after = jnp.where(lane == depth - 1, 0.0, pltpu.roll(field, depth - 1, 1))
    before = jnp.where(lane == 0, 0.0, pltpu.roll(field, 1, 1))
    return after, before


def shifted_y(field, row_after=0.0, row_before=0.0):
    rows = field.shape[0]
    row = lax.broadcasted_iota(jnp.int32, field.shape, 0)
    after = jnp.where(row == rows - 1, row_after, pltpu.roll(field, rows - 1, 0))
    before = jnp.where(row == 0, row_before, pltpu.roll(field, 1, 0))
    return after, before


def kernel(
    sizes,
    fringe_hbm,
    wind,
    adjoint,
    turbines,
    out,
    a_ext,
    w_ext,
    n_ext,
    b_ext,
    turb,
    coef,
    a_in,
    w_in,
    n_in,
    b_in,
    a_out,
    w_out,
    b_out,
    corner_in,
    corner_out,
    w_row,
    first_main,
    second_main,
    staged,
    main_rows,
    main_ends,
    rates,
    fringe,
    load_sem,
    send_sem,
    recv_sem,
):
    n_gx, n_gy, cells_x, cells_y = sizes
    cells_z = turb.shape[-1]
    dom, gx, gy = (lax.axis_index(a) for a in ("dom", "gx", "gy"))
    total = cells_x * n_gx
    reach = total // 4 - 1
    is_main = dom == 0
    in_fringe = jnp.logical_or(gx == n_gx - 1, gx * cells_x < reach)
    sends_forcing = jnp.logical_and(is_main, in_fringe)
    gets_forcing = jnp.logical_and(jnp.logical_not(is_main), in_fringe)
    up_x, down_x = lax.rem(gx + 1, n_gx), lax.rem(gx + n_gx - 1, n_gx)
    up_y, down_y = lax.rem(gy + 1, n_gy), lax.rem(gy + n_gy - 1, n_gy)
    places = ({"gx": up_x}, {"gx": down_x}, {"gy": up_y}, {"gy": down_y})
    partner = {"dom": 1 - dom}
    diagonal = tuple({"gx": x, "gy": y} for x in (up_x, down_x) for y in (up_y, down_y))

    def remote(src, dst, slot, device):
        return pltpu.make_async_remote_copy(
            src_ref=src,
            dst_ref=dst,
            send_sem=send_sem.at[slot],
            recv_sem=recv_sem.at[slot],
            device_id=device,
            device_id_type=pl.DeviceIdType.MESH,
        )

    inside = pl.ds(cells_y, cells_x * cells_y)
    inside_wind = pl.ds(2 * cells_y, cells_x * cells_y)
    load_fringe = pltpu.make_async_copy(fringe_hbm, fringe, load_sem.at[3])
    load_wind = pltpu.make_async_copy(wind, w_ext.at[:, inside_wind], load_sem.at[0])
    load_adjoint = pltpu.make_async_copy(adjoint, a_ext.at[:, inside], load_sem.at[1])
    load_turbines = pltpu.make_async_copy(turbines, turb, load_sem.at[2])

    barrier = pltpu.get_barrier_semaphore()
    for place in places + diagonal + (partner,):
        pl.semaphore_signal(
            barrier, inc=1, device_id=place, device_id_type=pl.DeviceIdType.MESH
        )
    load_wind.start()
    load_fringe.start()
    load_adjoint.start()
    load_turbines.start()
    pl.semaphore_wait(barrier, len(places) + len(diagonal) + 1)

    def slab(x):
        return pl.ds(pl.multiple_of(x * cells_y, 8), cells_y)

    def row(y, shift=0):
        return pl.ds(shift * cells_y + y, cells_x, stride=cells_y)

    def copies_x(slot, ext, last, first, depth):
        span = depth * cells_y
        pieces = (
            remote(last, ext.at[:, pl.ds(0, span)], slot, places[0]),
            remote(first, ext.at[:, pl.ds(cells_x * cells_y + span, span)], slot + 1, places[1]),
        )
        for piece in pieces:
            piece.start()
        return pieces

    def copies_y(slot, packed, sides):
        pieces = (
            remote(packed.at[0], sides.at[0], slot + 2, places[2]),
            remote(packed.at[1], sides.at[1], slot + 3, places[3]),
        )
        for piece in pieces:
            piece.start()
        return pieces

    span = 2 * cells_y
    wind_copies = copies_x(
        0,
        w_ext,
        wind.at[:, pl.ds((cells_x - 2) * cells_y, span)],
        wind.at[:, pl.ds(0, span)],
        2,
    )
    adjoint_copies = copies_x(
        4, a_ext, adjoint.at[:, slab(cells_x - 1)], adjoint.at[:, slab(0)], 1
    )
    load_wind.wait()
    for c in range(3):
        for j in range(2):
            w_out[0, c, j] = w_ext[c, row(cells_y - 1 - j, 2)]
            w_out[1, c, j] = w_ext[c, row(j, 2)]
    wind_copies += copies_y(0, w_out, w_in)
    corner_copies = []
    for q in range(4):
        x, y = (cells_x - 1, 0)[q // 2], (cells_y - 1, 0)[q % 2]
        for c in range(3):
            corner_out[q, c] = w_ext[c, pl.ds((x + 2) * cells_y + y, 1)]
        piece = remote(corner_out.at[q], corner_in.at[q], 8 + q, diagonal[q])
        piece.start()
        corner_copies.append(piece)
    load_adjoint.wait()
    for c in range(4):
        a_out[0, c] = a_ext[c, row(cells_y - 1, 1)]
        a_out[1, c] = a_ext[c, row(0, 1)]
    adjoint_copies += copies_y(4, a_out, a_in)
    first_forcing = remote(a_ext.at[pl.ds(0, 3), inside], first_main, 16, partner)

    @pl.when(sends_forcing)
    def _():
        first_forcing.start()

    def for_inner(body):
        inner = cells_x - 2
        size = max(g for g in range(1, GROUP + 1) if inner % g == 0)

        def several(i, carry):
            for k in range(size):
                body(1 + i * size + k)
            return carry

        lax.fori_loop(0, inner // size, several, 0)

    def for_slabs(body):
        body(0, lower=False)
        body(cells_x - 1, upper=False)
        for_inner(body)

    def neighbours(ext, c, x, lower=True, upper=True, base=1, rows=(0.0, 0.0)):
        here = ext[c, slab(x + base)]
        nothing = jnp.zeros_like(here)
        xp = ext[c, slab(x + base + 1)] if upper else nothing
        xm = ext[c, slab(x + base - 1)] if lower else nothing
        return (here, xp, xm, *shifted_y(here, *rows), *shifted_z(here))

    def strain(stencils):
        grads = []
        for _, xp, xm, yp, ym, zp, zm in stencils:
            grads.append((xp - xm, yp - ym, zp - zm))
        own = sum(grads[k][k] * grads[k][k] for k in range(3))
        xy = grads[0][1] + grads[1][0]
        xz = grads[0][2] + grads[2][0]
        yz = grads[1][2] + grads[2][1]
        return (0.5 * SMAG) * jnp.sqrt(2.0 * own + (xy * xy + xz * xz + yz * yz))

    def viscosity(x):
        n_ext[0, slab(x + 1)] = strain([neighbours(w_ext, c, x, base=2) for c in range(3)])

    for_inner(viscosity)
    for piece in wind_copies:
        piece.wait_recv()
    viscosity(0)
    viscosity(cells_x - 1)
    for side, y, inward in ((0, 0, 1), (1, cells_y - 1, cells_y - 2)):
        stencils = []
        for c in range(3):
            here, halo, near = w_ext[c, row(y, 2)], w_in[side, c, 0], w_ext[c, row(inward, 2)]
            along_y = (near, halo) if side == 0 else (halo, near)
            along_x = (w_ext[c, row(y, 3)], w_ext[c, row(y, 1)])
            stencils.append((here, *along_x, *along_y, *shifted_z(here)))
        n_ext[0, row(y, 1)] = strain(stencils)

    load_fringe.wait()
    position = gx * cells_x + lax.broadcasted_iota(jnp.int32, (cells_x, cells_z), 0)
    offset = position - fringe[0]
    offset = jnp.where(offset < 0, offset + total, offset)
    phase = math.pi * (offset.astype(jnp.float32) + 0.5) / fringe[1].astype(jnp.float32)
    sine = jnp.sin(phase)
    sign = jnp.where(is_main, -DT, DT)
    rates[...] = jnp.where(offset < fringe[1], sign * (RATE * sine * sine), 0.0)

    load_turbines.wait()
    drag_scale = jnp.where(is_main, DT * DRAG, 0.0)
    own_scale = jnp.where(is_main, 1.0, 0.0)

    def coefficients(x, **edges):
        u, v, w = (w_ext[c, slab(x + 2)] for c in range(3))
        nu, *faces = neighbours(n_ext, 0, x, **edges)
        nxp, nxm, nyp, nym, nzp, nzm = (face + nu for face in faces)
        speed = jnp.sqrt(u * u + v * v + w * w)
        drag = drag_scale * turb[slab(x)].astype(jnp.float32) * speed
        around = (nxp + nxm) + (nyp + nym) + (nzp + nzm)
        forcing = own_scale * rates[pl.ds(x, 1)]
        return (
            (1.0 + forcing) - H * around - drag,
            H * (nxp + u),
            H * (nxm - u),
            H * (nyp + v),
            H * (nym - v),
            H * (nzp + w),
            H * (nzm - w),
        )

    def advance(ext, weights, x, **edges):
        u, v, w = (w_ext[c, slab(x + 2)] for c in range(3))
        p, pxp, pxm, pyp, pym, pzp, pzm = neighbours(ext, 3, x, **edges)
        slopes = (pxp - pxm, pyp - pym, pzp - pzm)
        gain = u * slopes[0] + v * slopes[1] + w * slopes[2]
        results = []
        for c in range(3):
            stencil = neighbours(ext, c, x, **edges)
            gain = gain + (stencil[1 + 2 * c] - stencil[2 + 2 * c])
            new = sum(k * f for k, f in zip(weights, stencil))
            results.append(new + (SOUND_SQ * H) * slopes[c])
        results.append(p + H * gain)
        return results

    def first_step(x, **edges):
        weights = coefficients(x, **edges)
        for k, weight in enumerate(weights):
            coef[k, slab(x)] = weight
        for c, new in enumerate(advance(a_ext, weights, x, **edges)):
            b_ext[c, slab(x + 1)] = new
            if c < 3:
                staged[c, slab(x)] = new

    for_slabs(first_step)
    early_forcing = remote(staged, second_main, 17, partner)

    @pl.when(sends_forcing)
    def _():
        early_forcing.start()

    @pl.when(gets_forcing)
    def _():
        first_forcing.wait_recv()

        def add(x, **_):
            rate = rates[pl.ds(x, 1)]
            for c in range(3):
                b_ext[c, slab(x + 1)] += rate * first_main[c, slab(x)]

        for_slabs(add)

    def of_side(side):
        return lambda ext, sides, c: sides[side, c]

    def of_slab(x):
        return lambda ext, sides, c: ext[c, slab(x)]

    layers = (
        (slab(0), slab(1), slab(2), of_slab(0), 2, 0, -1.0),
        (slab(cells_x - 1), slab(cells_x), slab(cells_x + 1), of_slab(cells_x + 1), 1, 0, 1.0),
        (row(0), row(0, 1), row(0, 2), of_side(0), 4, 1, -1.0),
        (row(cells_y - 1), row(cells_y - 1, 1), row(cells_y - 1, 2), of_side(1), 3, 1, 1.0),
    )

    def halo_terms(weight, velocity, layer, along, sign):
        terms = [weight * layer[c] for c in range(3)]
        terms[along] = terms[along] + (sign * SOUND_SQ * H) * layer[3]
        terms.append((sign * H) * (velocity * layer[3] + layer[along]))
        return terms

    for piece in corner_copies:
        piece.wait_recv()
    for x, q in ((-1, 0), (cells_x, 2)):
        n_ext[0, slab(x + 1)] = strain(
            [
                neighbours(w_ext, c, x, base=2, rows=(corner_in[q + 1, c], corner_in[q, c]))
                for c in range(3)
            ]
        )
    for side, y in ((0, 0), (1, cells_y - 1)):
        stencils = []
        for c in range(3):
            here, far, near = w_in[side, c, 0], w_in[side, c, 1], w_ext[c, row(y, 2)]
            w_row[side, c, pl.ds(8, cells_x)] = here
            w_row[side, c, pl.ds(7, 1)] = corner_in[side, c]
            w_row[side, c, pl.ds(8 + cells_x, 1)] = corner_in[2 + side, c]
            along_x = (w_row[side, c, pl.ds(9, cells_x)], w_row[side, c, pl.ds(7, cells_x)])
            along_y = (near, far) if side == 0 else (far, near)
            stencils.append((here, *along_x, *along_y, *shifted_z(here)))
        n_in[side, 0] = strain(stencils)

    for piece in adjoint_copies:
        piece.wait_recv()
    for place, extended, windy, layer_of, k, along, sign in layers:
        nu = H * layer_of(n_ext, n_in, 0)
        weight = coef[k, place] + nu
        coef[k, place] = weight
        coef[0, place] -= nu
        layer = [layer_of(a_ext, a_in, c) for c in range(4)]
        terms = halo_terms(weight, w_ext[along, windy], layer, along, sign)
        for c in range(4):
            new = b_ext[c, extended] + terms[c]
            if c < 3:
                new = new - nu * a_ext[c, extended]
            b_ext[c, extended] = new
            if along == 1:
                b_out[1 if sign < 0 else 0, c] = new
    second_copies = copies_y(12, b_out, b_in)
    second_copies += copies_x(12, b_ext, b_ext.at[:, slab(cells_x)], b_ext.at[:, slab(1)], 1)
    velocities = pl.ds(0, 3)
    late_forcing = (
        remote(b_out.at[:, velocities], main_rows, 18, partner),
        remote(b_ext.at[velocities, slab(1)], main_ends.at[0], 19, partner),
        remote(b_ext.at[velocities, slab(cells_x)], main_ends.at[1], 20, partner),
    )

    @pl.when(sends_forcing)
    def _():
        for piece in late_forcing:
            piece.start()

    def second_step(x, **edges):
        weights = tuple(coef[k, slab(x)] for k in range(7))
        for c, new in enumerate(advance(b_ext, weights, x, **edges)):
            out[c, slab(x)] = new

    for_slabs(second_step)

    @pl.when(gets_forcing)
    def _():
        early_forcing.wait_recv()

        def add(x, **_):
            rate = rates[pl.ds(x, 1)]
            for c in range(3):
                out[c, slab(x)] += rate * second_main[c, slab(x)]

        for_slabs(add)

    for piece in second_copies:
        piece.wait_recv()
    for place, extended, windy, layer_of, k, along, sign in layers:
        layer = [layer_of(b_ext, b_in, c) for c in range(4)]
        terms = halo_terms(coef[k, place], w_ext[along, windy], layer, along, sign)
        for c in range(4):
            out[c, place] += terms[c]

    @pl.when(gets_forcing)
    def _():
        for piece in late_forcing:
            piece.wait_recv()
        for end, x in ((0, 0), (1, cells_x - 1)):
            rate = rates[pl.ds(x, 1)]
            for c in range(3):
                final = main_ends[end, c]
                out[c, slab(x)] += rate * (final - second_main[c, slab(x)])
                second_main[c, slab(x)] = final
        for side, y in ((0, cells_y - 1), (1, 0)):
            for c in range(3):
                out[c, row(y)] += rates[...] * (main_rows[side, c] - second_main[c, row(y)])

    for piece in (*wind_copies, *corner_copies, *adjoint_copies, *second_copies):
        piece.wait_send()

    @pl.when(sends_forcing)
    def _():
        first_forcing.wait_send()
        early_forcing.wait_send()
        for piece in late_forcing:
            piece.wait_send()


def on_device(wind, adjoint, turbines, fringe_range):
    _, _, cx, cy, cz = wind.shape
    f32 = jnp.float32
    sizes = (lax.axis_size("gx"), lax.axis_size("gy"), cx, cy)
    around, tile, wide = (cx + 2) * cy, cx * cy, (cx + 4) * cy
    later = pl.pallas_call(
        functools.partial(kernel, sizes),
        out_shape=pltpu.VMEM((4, tile, cz), f32),
        in_specs=[pl.BlockSpec(memory_space=pltpu.HBM)] * 4,
        out_specs=pl.BlockSpec(memory_space=pltpu.VMEM),
        scratch_shapes=[
            pltpu.VMEM((4, around, cz), f32),
            pltpu.VMEM((3, wide, cz), f32),
            pltpu.VMEM((1, around, cz), f32),
            pltpu.VMEM((4, around, cz), f32),
            pltpu.VMEM((tile, cz), jnp.int32),
            pltpu.VMEM((7, tile, cz), f32),
            pltpu.VMEM((2, 4, cx, cz), f32),
            pltpu.VMEM((2, 3, 2, cx, cz), f32),
            pltpu.VMEM((2, 1, cx, cz), f32),
            pltpu.VMEM((2, 4, cx, cz), f32),
            pltpu.VMEM((2, 4, cx, cz), f32),
            pltpu.VMEM((2, 3, 2, cx, cz), f32),
            pltpu.VMEM((2, 4, cx, cz), f32),
            pltpu.VMEM((4, 3, 1, cz), f32),
            pltpu.VMEM((4, 3, 1, cz), f32),
            pltpu.VMEM((2, 3, cx + 16, cz), f32),
            pltpu.VMEM((3, tile, cz), f32),
            pltpu.VMEM((3, tile, cz), f32),
            pltpu.VMEM((3, tile, cz), f32),
            pltpu.VMEM((2, 3, cx, cz), f32),
            pltpu.VMEM((2, 3, cy, cz), f32),
            pltpu.VMEM((cx, cz), f32),
            pltpu.SMEM((2,), jnp.int32),
            pltpu.SemaphoreType.DMA((4,)),
            pltpu.SemaphoreType.DMA((21,)),
            pltpu.SemaphoreType.DMA((21,)),
        ],
        compiler_params=pltpu.CompilerParams(
            collective_id=0, has_side_effects=True, vmem_limit_bytes=60 * 1024 * 1024
        ),
        name="adjoint_steps",
    )(
        fringe_range,
        wind.reshape(3, tile, cz),
        adjoint.reshape(4, tile, cz),
        turbines.reshape(tile, cz),
    )
    return later.reshape(adjoint.shape)


def solution(mesh):
    in_specs = (
        P("dom", None, "gx", "gy", None),
        P("dom", None, "gx", "gy", None),
        P("gx", "gy", None),
        P(),
    )
    out_specs = P("dom", None, "gx", "gy", None)
    return jax.shard_map(
        on_device, mesh=mesh, in_specs=in_specs, out_specs=out_specs, check_vma=False
    )
```

```python
import functools
import math

import jax
import jax.numpy as jnp
from jax import lax
from jax.experimental import pallas as pl
from jax.experimental.pallas import tpu as pltpu
from jax.sharding import PartitionSpec as P

DT = 0.1
SMAG = 0.1
SOUND_SQ = 4.0
DRAG = 1.0
RATE = 3.0
H = 0.5 * DT
GROUP = 14


def shifted_z(field):
    depth = field.shape[-1]
    lane = lax.broadcasted_iota(jnp.int32, field.shape, 1)
    after = jnp.where(lane == depth - 1, 0.0, pltpu.roll(field, depth - 1, 1))
    before = jnp.where(lane == 0, 0.0, pltpu.roll(field, 1, 1))
    return after, before


def shifted_y(field, row_after=0.0, row_before=0.0):
    rows = field.shape[0]
    row = lax.broadcasted_iota(jnp.int32, field.shape, 0)
    after = jnp.where(row == rows - 1, row_after, pltpu.roll(field, rows - 1, 0))
    before = jnp.where(row == 0, row_before, pltpu.roll(field, 1, 0))
    return after, before


def kernel(
    sizes,
    fringe_hbm,
    wind,
    adjoint,
    turbines,
    out,
    a_ext,
    w_ext,
    n_ext,
    b_ext,
    turb,
    coef,
    a_in,
    w_in,
    n_in,
    b_in,
    a_out,
    w_out,
    b_out,
    corner_in,
    corner_out,
    w_row,
    first_main,
    second_main,
    rates,
    fringe,
    load_sem,
    send_sem,
    recv_sem,
):
    n_gx, n_gy, cells_x, cells_y = sizes
    cells_z = turb.shape[-1]
    dom, gx, gy = (lax.axis_index(a) for a in ("dom", "gx", "gy"))
    total = cells_x * n_gx
    reach = total // 4 - 1
    is_main = dom == 0
    in_fringe = jnp.logical_or(gx == n_gx - 1, gx * cells_x < reach)
    sends_forcing = jnp.logical_and(is_main, in_fringe)
    gets_forcing = jnp.logical_and(jnp.logical_not(is_main), in_fringe)
    up_x, down_x = lax.rem(gx + 1, n_gx), lax.rem(gx + n_gx - 1, n_gx)
    up_y, down_y = lax.rem(gy + 1, n_gy), lax.rem(gy + n_gy - 1, n_gy)
    places = ({"gx": up_x}, {"gx": down_x}, {"gy": up_y}, {"gy": down_y})
    partner = {"dom": 1 - dom}
    diagonal = tuple({"gx": x, "gy": y} for x in (up_x, down_x) for y in (up_y, down_y))

    def remote(src, dst, slot, device):
        return pltpu.make_async_remote_copy(
            src_ref=src,
            dst_ref=dst,
            send_sem=send_sem.at[slot],
            recv_sem=recv_sem.at[slot],
            device_id=device,
            device_id_type=pl.DeviceIdType.MESH,
        )

    inside = pl.ds(cells_y, cells_x * cells_y)
    inside_wind = pl.ds(2 * cells_y, cells_x * cells_y)
    load_fringe = pltpu.make_async_copy(fringe_hbm, fringe, load_sem.at[3])
    load_wind = pltpu.make_async_copy(wind, w_ext.at[:, inside_wind], load_sem.at[0])
    load_adjoint = pltpu.make_async_copy(adjoint, a_ext.at[:, inside], load_sem.at[1])
    load_turbines = pltpu.make_async_copy(turbines, turb, load_sem.at[2])

    load_wind.start()
    load_adjoint.start()
    barrier = pltpu.get_barrier_semaphore()
    for place in places + diagonal + (partner,):
        pl.semaphore_signal(
            barrier, inc=1, device_id=place, device_id_type=pl.DeviceIdType.MESH
        )
    load_fringe.start()
    load_turbines.start()
    pl.semaphore_wait(barrier, len(places) + len(diagonal) + 1)

    def slab(x):
        return pl.ds(pl.multiple_of(x * cells_y, 8), cells_y)

    def row(y, shift=0):
        return pl.ds(shift * cells_y + y, cells_x, stride=cells_y)

    def copies_x(slot, ext, last, first, depth):
        span = depth * cells_y
        pieces = (
            remote(last, ext.at[:, pl.ds(0, span)], slot, places[0]),
            remote(first, ext.at[:, pl.ds(cells_x * cells_y + span, span)], slot + 1, places[1]),
        )
        for piece in pieces:
            piece.start()
        return pieces

    def copies_y(slot, packed, sides):
        pieces = (
            remote(packed.at[0], sides.at[0], slot + 2, places[2]),
            remote(packed.at[1], sides.at[1], slot + 3, places[3]),
        )
        for piece in pieces:
            piece.start()
        return pieces

    span = 2 * cells_y
    wind_copies = copies_x(
        0,
        w_ext,
        wind.at[:, pl.ds((cells_x - 2) * cells_y, span)],
        wind.at[:, pl.ds(0, span)],
        2,
    )
    adjoint_copies = copies_x(
        4, a_ext, adjoint.at[:, slab(cells_x - 1)], adjoint.at[:, slab(0)], 1
    )
    load_wind.wait()
    for c in range(3):
        for j in range(2):
            w_out[0, c, j] = w_ext[c, row(cells_y - 1 - j, 2)]
            w_out[1, c, j] = w_ext[c, row(j, 2)]
    wind_copies += copies_y(0, w_out, w_in)
    corner_copies = []
    for q in range(4):
        x, y = (cells_x - 1, 0)[q // 2], (cells_y - 1, 0)[q % 2]
        for c in range(3):
            corner_out[q, c] = w_ext[c, pl.ds((x + 2) * cells_y + y, 1)]
        piece = remote(corner_out.at[q], corner_in.at[q], 8 + q, diagonal[q])
        piece.start()
        corner_copies.append(piece)
    load_adjoint.wait()
    for c in range(4):
        a_out[0, c] = a_ext[c, row(cells_y - 1, 1)]
        a_out[1, c] = a_ext[c, row(0, 1)]
    adjoint_copies += copies_y(4, a_out, a_in)
    first_forcing = remote(a_ext.at[pl.ds(0, 3), inside], first_main, 16, partner)

    @pl.when(sends_forcing)
    def _():
        first_forcing.start()

    def for_inner(body):
        inner = cells_x - 2
        size = max(g for g in range(1, GROUP + 1) if inner % g == 0)

        def several(i, carry):
            for k in range(size):
                body(1 + i * size + k)
            return carry

        lax.fori_loop(0, inner // size, several, 0)

    def for_slabs(body):
        body(0, lower=False)
        body(cells_x - 1, upper=False)
        for_inner(body)

    def neighbours(ext, c, x, lower=True, upper=True, base=1, rows=(0.0, 0.0)):
        here = ext[c, slab(x + base)]
        nothing = jnp.zeros_like(here)
        xp = ext[c, slab(x + base + 1)] if upper else nothing
        xm = ext[c, slab(x + base - 1)] if lower else nothing
        return (here, xp, xm, *shifted_y(here, *rows), *shifted_z(here))

    def strain(stencils):
        grads = []
        for _, xp, xm, yp, ym, zp, zm in stencils:
            grads.append((xp - xm, yp - ym, zp - zm))
        own = sum(grads[k][k] * grads[k][k] for k in range(3))
        xy = grads[0][1] + grads[1][0]
        xz = grads[0][2] + grads[2][0]
        yz = grads[1][2] + grads[2][1]
        return (0.5 * SMAG) * jnp.sqrt(2.0 * own + (xy * xy + xz * xz + yz * yz))

    def viscosity(x):
        n_ext[0, slab(x + 1)] = strain([neighbours(w_ext, c, x, base=2) for c in range(3)])

    for_inner(viscosity)
    for piece in wind_copies:
        piece.wait_recv()
    viscosity(0)
    viscosity(cells_x - 1)
    for side, y, inward in ((0, 0, 1), (1, cells_y - 1, cells_y - 2)):
        stencils = []
        for c in range(3):
            here, halo, near = w_ext[c, row(y, 2)], w_in[side, c, 0], w_ext[c, row(inward, 2)]
            along_y = (near, halo) if side == 0 else (halo, near)
            along_x = (w_ext[c, row(y, 3)], w_ext[c, row(y, 1)])
            stencils.append((here, *along_x, *along_y, *shifted_z(here)))
        n_ext[0, row(y, 1)] = strain(stencils)

    load_fringe.wait()
    position = gx * cells_x + lax.broadcasted_iota(jnp.int32, (cells_x, cells_z), 0)
    offset = position - fringe[0]
    offset = jnp.where(offset < 0, offset + total, offset)
    phase = math.pi * (offset.astype(jnp.float32) + 0.5) / fringe[1].astype(jnp.float32)
    sine = jnp.sin(phase)
    sign = jnp.where(is_main, -DT, DT)
    rates[...] = jnp.where(offset < fringe[1], sign * (RATE * sine * sine), 0.0)

    load_turbines.wait()
    drag_scale = jnp.where(is_main, DT * DRAG, 0.0)
    own_scale = jnp.where(is_main, 1.0, 0.0)

    def coefficients(x, **edges):
        u, v, w = (w_ext[c, slab(x + 2)] for c in range(3))
        nu, *faces = neighbours(n_ext, 0, x, **edges)
        nxp, nxm, nyp, nym, nzp, nzm = (face + nu for face in faces)
        speed = jnp.sqrt(u * u + v * v + w * w)
        drag = drag_scale * turb[slab(x)].astype(jnp.float32) * speed
        around = (nxp + nxm) + (nyp + nym) + (nzp + nzm)
        forcing = own_scale * rates[pl.ds(x, 1)]
        return (
            (1.0 + forcing) - H * around - drag,
            H * (nxp + u),
            H * (nxm - u),
            H * (nyp + v),
            H * (nym - v),
            H * (nzp + w),
            H * (nzm - w),
        )

    def advance(ext, weights, x, **edges):
        u, v, w = (w_ext[c, slab(x + 2)] for c in range(3))
        p, pxp, pxm, pyp, pym, pzp, pzm = neighbours(ext, 3, x, **edges)
        slopes = (pxp - pxm, pyp - pym, pzp - pzm)
        gain = u * slopes[0] + v * slopes[1] + w * slopes[2]
        results = []
        for c in range(3):
            stencil = neighbours(ext, c, x, **edges)
            gain = gain + (stencil[1 + 2 * c] - stencil[2 + 2 * c])
            new = sum(k * f for k, f in zip(weights, stencil))
            results.append(new + (SOUND_SQ * H) * slopes[c])
        results.append(p + H * gain)
        return results

    def first_step(x, **edges):
        weights = coefficients(x, **edges)
        for k, weight in enumerate(weights):
            coef[k, slab(x)] = weight
        for c, new in enumerate(advance(a_ext, weights, x, **edges)):
            b_ext[c, slab(x + 1)] = new

    for_slabs(first_step)

    @pl.when(gets_forcing)
    def _():
        first_forcing.wait_recv()

        def add(x, **_):
            rate = rates[pl.ds(x, 1)]
            for c in range(3):
                b_ext[c, slab(x + 1)] += rate * first_main[c, slab(x)]

        for_slabs(add)

    def of_side(side):
        return lambda ext, sides, c: sides[side, c]

    def of_slab(x):
        return lambda ext, sides, c: ext[c, slab(x)]

    layers = (
        (slab(0), slab(1), slab(2), of_slab(0), 2, 0, -1.0),
        (slab(cells_x - 1), slab(cells_x), slab(cells_x + 1), of_slab(cells_x + 1), 1, 0, 1.0),
        (row(0), row(0, 1), row(0, 2), of_side(0), 4, 1, -1.0),
        (row(cells_y - 1), row(cells_y - 1, 1), row(cells_y - 1, 2), of_side(1), 3, 1, 1.0),
    )

    def halo_terms(weight, velocity, layer, along, sign):
        terms = [weight * layer[c] for c in range(3)]
        terms[along] = terms[along] + (sign * SOUND_SQ * H) * layer[3]
        terms.append((sign * H) * (velocity * layer[3] + layer[along]))
        return terms

    for piece in corner_copies:
        piece.wait_recv()
    for x, q in ((-1, 0), (cells_x, 2)):
        n_ext[0, slab(x + 1)] = strain(
            [
                neighbours(w_ext, c, x, base=2, rows=(corner_in[q + 1, c], corner_in[q, c]))
                for c in range(3)
            ]
        )
    for side, y in ((0, 0), (1, cells_y - 1)):
        stencils = []
        for c in range(3):
            here, far, near = w_in[side, c, 0], w_in[side, c, 1], w_ext[c, row(y, 2)]
            w_row[side, c, pl.ds(8, cells_x)] = here
            w_row[side, c, pl.ds(7, 1)] = corner_in[side, c]
            w_row[side, c, pl.ds(8 + cells_x, 1)] = corner_in[2 + side, c]
            along_x = (w_row[side, c, pl.ds(9, cells_x)], w_row[side, c, pl.ds(7, cells_x)])
            along_y = (near, far) if side == 0 else (far, near)
            stencils.append((here, *along_x, *along_y, *shifted_z(here)))
        n_in[side, 0] = strain(stencils)

    for piece in adjoint_copies:
        piece.wait_recv()
    for place, extended, windy, layer_of, k, along, sign in layers:
        nu = H * layer_of(n_ext, n_in, 0)
        weight = coef[k, place] + nu
        coef[k, place] = weight
        coef[0, place] -= nu
        layer = [layer_of(a_ext, a_in, c) for c in range(4)]
        terms = halo_terms(weight, w_ext[along, windy], layer, along, sign)
        for c in range(4):
            new = b_ext[c, extended] + terms[c]
            if c < 3:
                new = new - nu * a_ext[c, extended]
            b_ext[c, extended] = new
            if along == 1:
                b_out[1 if sign < 0 else 0, c] = new
    second_copies = copies_y(12, b_out, b_in)
    second_copies += copies_x(12, b_ext, b_ext.at[:, slab(cells_x)], b_ext.at[:, slab(1)], 1)
    second_forcing = remote(b_ext.at[pl.ds(0, 3), inside], second_main, 17, partner)

    @pl.when(sends_forcing)
    def _():
        second_forcing.start()

    def second_step(x, **edges):
        weights = tuple(coef[k, slab(x)] for k in range(7))
        for c, new in enumerate(advance(b_ext, weights, x, **edges)):
            out[c, slab(x)] = new

    for_slabs(second_step)

    for piece in second_copies:
        piece.wait_recv()
    for place, extended, windy, layer_of, k, along, sign in layers:
        layer = [layer_of(b_ext, b_in, c) for c in range(4)]
        terms = halo_terms(coef[k, place], w_ext[along, windy], layer, along, sign)
        for c in range(4):
            out[c, place] += terms[c]

    @pl.when(gets_forcing)
    def _():
        second_forcing.wait_recv()

        def add(x, **_):
            rate = rates[pl.ds(x, 1)]
            for c in range(3):
                out[c, slab(x)] += rate * second_main[c, slab(x)]

        for_slabs(add)

    for piece in (*wind_copies, *corner_copies, *adjoint_copies, *second_copies):
        piece.wait_send()

    @pl.when(sends_forcing)
    def _():
        first_forcing.wait_send()
        second_forcing.wait_send()


def on_device(wind, adjoint, turbines, fringe_range):
    _, _, cx, cy, cz = wind.shape
    f32 = jnp.float32
    sizes = (lax.axis_size("gx"), lax.axis_size("gy"), cx, cy)
    around, tile, wide = (cx + 2) * cy, cx * cy, (cx + 4) * cy
    later = pl.pallas_call(
        functools.partial(kernel, sizes),
        out_shape=pltpu.VMEM((4, tile, cz), f32),
        in_specs=[pl.BlockSpec(memory_space=pltpu.HBM)] * 4,
        out_specs=pl.BlockSpec(memory_space=pltpu.VMEM),
        scratch_shapes=[
            pltpu.VMEM((4, around, cz), f32),
            pltpu.VMEM((3, wide, cz), f32),
            pltpu.VMEM((1, around, cz), f32),
            pltpu.VMEM((4, around, cz), f32),
            pltpu.VMEM((tile, cz), jnp.int32),
            pltpu.VMEM((7, tile, cz), f32),
            pltpu.VMEM((2, 4, cx, cz), f32),
            pltpu.VMEM((2, 3, 2, cx, cz), f32),
            pltpu.VMEM((2, 1, cx, cz), f32),
            pltpu.VMEM((2, 4, cx, cz), f32),
            pltpu.VMEM((2, 4, cx, cz), f32),
            pltpu.VMEM((2, 3, 2, cx, cz), f32),
            pltpu.VMEM((2, 4, cx, cz), f32),
            pltpu.VMEM((4, 3, 1, cz), f32),
            pltpu.VMEM((4, 3, 1, cz), f32),
            pltpu.VMEM((2, 3, cx + 16, cz), f32),
            pltpu.VMEM((3, tile, cz), f32),
            pltpu.VMEM((3, tile, cz), f32),
            pltpu.VMEM((cx, cz), f32),
            pltpu.SMEM((2,), jnp.int32),
            pltpu.SemaphoreType.DMA((4,)),
            pltpu.SemaphoreType.DMA((18,)),
            pltpu.SemaphoreType.DMA((18,)),
        ],
        compiler_params=pltpu.CompilerParams(
            collective_id=0, has_side_effects=True, vmem_limit_bytes=60 * 1024 * 1024
        ),
        name="adjoint_steps",
    )(
        fringe_range,
        wind.reshape(3, tile, cz),
        adjoint.reshape(4, tile, cz),
        turbines.reshape(tile, cz),
    )
    return later.reshape(adjoint.shape)


def solution(mesh):
    in_specs = (
        P("dom", None, "gx", "gy", None),
        P("dom", None, "gx", "gy", None),
        P("gx", "gy", None),
        P(),
    )
    out_specs = P("dom", None, "gx", "gy", None)
    return jax.shard_map(
        on_device, mesh=mesh, in_specs=in_specs, out_specs=out_specs, check_vma=False
    )
```

```python
import functools
import math

import jax
import jax.numpy as jnp
from jax import lax
from jax.experimental import pallas as pl
from jax.experimental.pallas import tpu as pltpu
from jax.sharding import PartitionSpec as P

DT = 0.1
SMAG = 0.1
SOUND_SQ = 4.0
DRAG = 1.0
RATE = 3.0
H = 0.5 * DT
GROUP = 14


def shifted_z(field):
    depth = field.shape[-1]
    lane = lax.broadcasted_iota(jnp.int32, field.shape, 1)
    after = jnp.where(lane == depth - 1, 0.0, pltpu.roll(field, depth - 1, 1))
    before = jnp.where(lane == 0, 0.0, pltpu.roll(field, 1, 1))
    return after, before


def shifted_y(field, row_after=0.0, row_before=0.0):
    rows = field.shape[0]
    row = lax.broadcasted_iota(jnp.int32, field.shape, 0)
    after = jnp.where(row == rows - 1, row_after, pltpu.roll(field, rows - 1, 0))
    before = jnp.where(row == 0, row_before, pltpu.roll(field, 1, 0))
    return after, before


def kernel(
    sizes,
    fringe_hbm,
    wind,
    adjoint,
    turbines,
    out,
    a_ext,
    w_ext,
    n_ext,
    b_ext,
    turb,
    coef,
    a_in,
    w_in,
    n_in,
    b_in,
    a_out,
    w_out,
    b_out,
    corner_in,
    corner_out,
    w_row,
    first_main,
    second_main,
    rates,
    fringe,
    load_sem,
    send_sem,
    recv_sem,
):
    n_gx, n_gy, cells_x, cells_y = sizes
    cells_z = turb.shape[-1]
    dom, gx, gy = (lax.axis_index(a) for a in ("dom", "gx", "gy"))
    total = cells_x * n_gx
    reach = total // 4 - 1
    is_main = dom == 0
    in_fringe = jnp.logical_or(gx == n_gx - 1, gx * cells_x < reach)
    sends_forcing = jnp.logical_and(is_main, in_fringe)
    gets_forcing = jnp.logical_and(jnp.logical_not(is_main), in_fringe)
    up_x, down_x = lax.rem(gx + 1, n_gx), lax.rem(gx + n_gx - 1, n_gx)
    up_y, down_y = lax.rem(gy + 1, n_gy), lax.rem(gy + n_gy - 1, n_gy)
    places = ({"gx": up_x}, {"gx": down_x}, {"gy": up_y}, {"gy": down_y})
    partner = {"dom": 1 - dom}
    diagonal = tuple({"gx": x, "gy": y} for x in (up_x, down_x) for y in (up_y, down_y))

    def remote(src, dst, slot, device):
        return pltpu.make_async_remote_copy(
            src_ref=src,
            dst_ref=dst,
            send_sem=send_sem.at[slot],
            recv_sem=recv_sem.at[slot],
            device_id=device,
            device_id_type=pl.DeviceIdType.MESH,
        )

    inside = pl.ds(cells_y, cells_x * cells_y)
    inside_wind = pl.ds(2 * cells_y, cells_x * cells_y)
    load_fringe = pltpu.make_async_copy(fringe_hbm, fringe, load_sem.at[3])
    load_wind = pltpu.make_async_copy(wind, w_ext.at[:, inside_wind], load_sem.at[0])
    load_adjoint = pltpu.make_async_copy(adjoint, a_ext.at[:, inside], load_sem.at[1])
    load_turbines = pltpu.make_async_copy(turbines, turb, load_sem.at[2])

    load_wind.start()
    load_adjoint.start()
    barrier = pltpu.get_barrier_semaphore()
    for place in places + diagonal + (partner,):
        pl.semaphore_signal(
            barrier, inc=1, device_id=place, device_id_type=pl.DeviceIdType.MESH
        )
    load_fringe.start()
    load_turbines.start()
    pl.semaphore_wait(barrier, len(places) + len(diagonal) + 1)

    def slab(x):
        return pl.ds(pl.multiple_of(x * cells_y, 8), cells_y)

    def row(y, shift=0):
        return pl.ds(shift * cells_y + y, cells_x, stride=cells_y)

    def copies_x(slot, ext, last, first, depth):
        span = depth * cells_y
        pieces = (
            remote(last, ext.at[:, pl.ds(0, span)], slot, places[0]),
            remote(first, ext.at[:, pl.ds(cells_x * cells_y + span, span)], slot + 1, places[1]),
        )
        for piece in pieces:
            piece.start()
        return pieces

    def copies_y(slot, packed, sides):
        pieces = (
            remote(packed.at[0], sides.at[0], slot + 2, places[2]),
            remote(packed.at[1], sides.at[1], slot + 3, places[3]),
        )
        for piece in pieces:
            piece.start()
        return pieces

    span = 2 * cells_y
    wind_copies = copies_x(
        0,
        w_ext,
        wind.at[:, pl.ds((cells_x - 2) * cells_y, span)],
        wind.at[:, pl.ds(0, span)],
        2,
    )
    load_wind.wait()
    for c in range(3):
        for j in range(2):
            w_out[0, c, j] = w_ext[c, row(cells_y - 1 - j, 2)]
            w_out[1, c, j] = w_ext[c, row(j, 2)]
    wind_copies += copies_y(0, w_out, w_in)
    adjoint_copies = copies_x(
        4, a_ext, adjoint.at[:, slab(cells_x - 1)], adjoint.at[:, slab(0)], 1
    )
    load_adjoint.wait()
    for c in range(4):
        a_out[0, c] = a_ext[c, row(cells_y - 1, 1)]
        a_out[1, c] = a_ext[c, row(0, 1)]
    adjoint_copies += copies_y(4, a_out, a_in)
    corner_copies = []
    for q in range(4):
        x, y = (cells_x - 1, 0)[q // 2], (cells_y - 1, 0)[q % 2]
        for c in range(3):
            corner_out[q, c] = w_ext[c, pl.ds((x + 2) * cells_y + y, 1)]
        piece = remote(corner_out.at[q], corner_in.at[q], 8 + q, diagonal[q])
        piece.start()
        corner_copies.append(piece)
    first_forcing = remote(a_ext.at[pl.ds(0, 3), inside], first_main, 16, partner)

    @pl.when(sends_forcing)
    def _():
        first_forcing.start()

    def for_inner(body):
        inner = cells_x - 2
        size = max(g for g in range(1, GROUP + 1) if inner % g == 0)

        def several(i, carry):
            for k in range(size):
                body(1 + i * size + k)
            return carry

        lax.fori_loop(0, inner // size, several, 0)

    def for_slabs(body):
        body(0, lower=False)
        body(cells_x - 1, upper=False)
        for_inner(body)

    def neighbours(ext, c, x, lower=True, upper=True, base=1, rows=(0.0, 0.0)):
        here = ext[c, slab(x + base)]
        nothing = jnp.zeros_like(here)
        xp = ext[c, slab(x + base + 1)] if upper else nothing
        xm = ext[c, slab(x + base - 1)] if lower else nothing
        return (here, xp, xm, *shifted_y(here, *rows), *shifted_z(here))

    def strain(stencils):
        grads = []
        for _, xp, xm, yp, ym, zp, zm in stencils:
            grads.append((xp - xm, yp - ym, zp - zm))
        own = sum(grads[k][k] * grads[k][k] for k in range(3))
        xy = grads[0][1] + grads[1][0]
        xz = grads[0][2] + grads[2][0]
        yz = grads[1][2] + grads[2][1]
        return (0.5 * SMAG) * jnp.sqrt(2.0 * own + (xy * xy + xz * xz + yz * yz))

    def viscosity(x):
        n_ext[0, slab(x + 1)] = strain([neighbours(w_ext, c, x, base=2) for c in range(3)])

    for_inner(viscosity)
    for piece in wind_copies:
        piece.wait_recv()
    viscosity(0)
    viscosity(cells_x - 1)
    for side, y, inward in ((0, 0, 1), (1, cells_y - 1, cells_y - 2)):
        stencils = []
        for c in range(3):
            here, halo, near = w_ext[c, row(y, 2)], w_in[side, c, 0], w_ext[c, row(inward, 2)]
            along_y = (near, halo) if side == 0 else (halo, near)
            along_x = (w_ext[c, row(y, 3)], w_ext[c, row(y, 1)])
            stencils.append((here, *along_x, *along_y, *shifted_z(here)))
        n_ext[0, row(y, 1)] = strain(stencils)

    load_fringe.wait()
    position = gx * cells_x + lax.broadcasted_iota(jnp.int32, (cells_x, cells_z), 0)
    offset = position - fringe[0]
    offset = jnp.where(offset < 0, offset + total, offset)
    phase = math.pi * (offset.astype(jnp.float32) + 0.5) / fringe[1].astype(jnp.float32)
    sine = jnp.sin(phase)
    sign = jnp.where(is_main, -DT, DT)
    rates[...] = jnp.where(offset < fringe[1], sign * (RATE * sine * sine), 0.0)

    load_turbines.wait()
    drag_scale = jnp.where(is_main, DT * DRAG, 0.0)
    own_scale = jnp.where(is_main, 1.0, 0.0)

    def coefficients(x, **edges):
        u, v, w = (w_ext[c, slab(x + 2)] for c in range(3))
        nu, *faces = neighbours(n_ext, 0, x, **edges)
        nxp, nxm, nyp, nym, nzp, nzm = (face + nu for face in faces)
        speed = jnp.sqrt(u * u + v * v + w * w)
        drag = drag_scale * turb[slab(x)].astype(jnp.float32) * speed
        around = (nxp + nxm) + (nyp + nym) + (nzp + nzm)
        forcing = own_scale * rates[pl.ds(x, 1)]
        return (
            (1.0 + forcing) - H * around - drag,
            H * (nxp + u),
            H * (nxm - u),
            H * (nyp + v),
            H * (nym - v),
            H * (nzp + w),
            H * (nzm - w),
        )

    def advance(ext, weights, x, **edges):
        u, v, w = (w_ext[c, slab(x + 2)] for c in range(3))
        p, pxp, pxm, pyp, pym, pzp, pzm = neighbours(ext, 3, x, **edges)
        slopes = (pxp - pxm, pyp - pym, pzp - pzm)
        gain = u * slopes[0] + v * slopes[1] + w * slopes[2]
        results = []
        for c in range(3):
            stencil = neighbours(ext, c, x, **edges)
            gain = gain + (stencil[1 + 2 * c] - stencil[2 + 2 * c])
            new = sum(k * f for k, f in zip(weights, stencil))
            results.append(new + (SOUND_SQ * H) * slopes[c])
        results.append(p + H * gain)
        return results

    def first_step(x, **edges):
        weights = coefficients(x, **edges)
        for k, weight in enumerate(weights):
            coef[k, slab(x)] = weight
        for c, new in enumerate(advance(a_ext, weights, x, **edges)):
            b_ext[c, slab(x + 1)] = new

    for_slabs(first_step)

    @pl.when(gets_forcing)
    def _():
        first_forcing.wait_recv()

        def add(x, **_):
            rate = rates[pl.ds(x, 1)]
            for c in range(3):
                b_ext[c, slab(x + 1)] += rate * first_main[c, slab(x)]

        for_slabs(add)

    def of_side(side):
        return lambda ext, sides, c: sides[side, c]

    def of_slab(x):
        return lambda ext, sides, c: ext[c, slab(x)]

    layers = (
        (slab(0), slab(1), slab(2), of_slab(0), 2, 0, -1.0),
        (slab(cells_x - 1), slab(cells_x), slab(cells_x + 1), of_slab(cells_x + 1), 1, 0, 1.0),
        (row(0), row(0, 1), row(0, 2), of_side(0), 4, 1, -1.0),
        (row(cells_y - 1), row(cells_y - 1, 1), row(cells_y - 1, 2), of_side(1), 3, 1, 1.0),
    )

    def halo_terms(weight, velocity, layer, along, sign):
        terms = [weight * layer[c] for c in range(3)]
        terms[along] = terms[along] + (sign * SOUND_SQ * H) * layer[3]
        terms.append((sign * H) * (velocity * layer[3] + layer[along]))
        return terms

    for piece in corner_copies:
        piece.wait_recv()
    for x, q in ((-1, 0), (cells_x, 2)):
        n_ext[0, slab(x + 1)] = strain(
            [
                neighbours(w_ext, c, x, base=2, rows=(corner_in[q + 1, c], corner_in[q, c]))
                for c in range(3)
            ]
        )
    for side, y in ((0, 0), (1, cells_y - 1)):
        stencils = []
        for c in range(3):
            here, far, near = w_in[side, c, 0], w_in[side, c, 1], w_ext[c, row(y, 2)]
            w_row[side, c, pl.ds(8, cells_x)] = here
            w_row[side, c, pl.ds(7, 1)] = corner_in[side, c]
            w_row[side, c, pl.ds(8 + cells_x, 1)] = corner_in[2 + side, c]
            along_x = (w_row[side, c, pl.ds(9, cells_x)], w_row[side, c, pl.ds(7, cells_x)])
            along_y = (near, far) if side == 0 else (far, near)
            stencils.append((here, *along_x, *along_y, *shifted_z(here)))
        n_in[side, 0] = strain(stencils)

    for piece in adjoint_copies:
        piece.wait_recv()
    for place, extended, windy, layer_of, k, along, sign in layers:
        nu = H * layer_of(n_ext, n_in, 0)
        weight = coef[k, place] + nu
        coef[k, place] = weight
        coef[0, place] -= nu
        layer = [layer_of(a_ext, a_in, c) for c in range(4)]
        terms = halo_terms(weight, w_ext[along, windy], layer, along, sign)
        for c in range(4):
            new = b_ext[c, extended] + terms[c]
            if c < 3:
                new = new - nu * a_ext[c, extended]
            b_ext[c, extended] = new
            if along == 1:
                b_out[1 if sign < 0 else 0, c] = new
    second_copies = copies_y(12, b_out, b_in)
    second_copies += copies_x(12, b_ext, b_ext.at[:, slab(cells_x)], b_ext.at[:, slab(1)], 1)
    second_forcing = remote(b_ext.at[pl.ds(0, 3), inside], second_main, 17, partner)

    @pl.when(sends_forcing)
    def _():
        second_forcing.start()

    def second_step(x, **edges):
        weights = tuple(coef[k, slab(x)] for k in range(7))
        for c, new in enumerate(advance(b_ext, weights, x, **edges)):
            out[c, slab(x)] = new

    for_slabs(second_step)

    for piece in second_copies:
        piece.wait_recv()
    for place, extended, windy, layer_of, k, along, sign in layers:
        layer = [layer_of(b_ext, b_in, c) for c in range(4)]
        terms = halo_terms(coef[k, place], w_ext[along, windy], layer, along, sign)
        for c in range(4):
            out[c, place] += terms[c]

    @pl.when(gets_forcing)
    def _():
        second_forcing.wait_recv()

        def add(x, **_):
            rate = rates[pl.ds(x, 1)]
            for c in range(3):
                out[c, slab(x)] += rate * second_main[c, slab(x)]

        for_slabs(add)

    for piece in (*wind_copies, *corner_copies, *adjoint_copies, *second_copies):
        piece.wait_send()

    @pl.when(sends_forcing)
    def _():
        first_forcing.wait_send()
        second_forcing.wait_send()


def on_device(wind, adjoint, turbines, fringe_range):
    _, _, cx, cy, cz = wind.shape
    f32 = jnp.float32
    sizes = (lax.axis_size("gx"), lax.axis_size("gy"), cx, cy)
    around, tile, wide = (cx + 2) * cy, cx * cy, (cx + 4) * cy
    later = pl.pallas_call(
        functools.partial(kernel, sizes),
        out_shape=pltpu.VMEM((4, tile, cz), f32),
        in_specs=[pl.BlockSpec(memory_space=pltpu.HBM)] * 4,
        out_specs=pl.BlockSpec(memory_space=pltpu.VMEM),
        scratch_shapes=[
            pltpu.VMEM((4, around, cz), f32),
            pltpu.VMEM((3, wide, cz), f32),
            pltpu.VMEM((1, around, cz), f32),
            pltpu.VMEM((4, around, cz), f32),
            pltpu.VMEM((tile, cz), jnp.int32),
            pltpu.VMEM((7, tile, cz), f32),
            pltpu.VMEM((2, 4, cx, cz), f32),
            pltpu.VMEM((2, 3, 2, cx, cz), f32),
            pltpu.VMEM((2, 1, cx, cz), f32),
            pltpu.VMEM((2, 4, cx, cz), f32),
            pltpu.VMEM((2, 4, cx, cz), f32),
            pltpu.VMEM((2, 3, 2, cx, cz), f32),
            pltpu.VMEM((2, 4, cx, cz), f32),
            pltpu.VMEM((4, 3, 1, cz), f32),
            pltpu.VMEM((4, 3, 1, cz), f32),
            pltpu.VMEM((2, 3, cx + 16, cz), f32),
            pltpu.VMEM((3, tile, cz), f32),
            pltpu.VMEM((3, tile, cz), f32),
            pltpu.VMEM((cx, cz), f32),
            pltpu.SMEM((2,), jnp.int32),
            pltpu.SemaphoreType.DMA((4,)),
            pltpu.SemaphoreType.DMA((18,)),
            pltpu.SemaphoreType.DMA((18,)),
        ],
        compiler_params=pltpu.CompilerParams(
            collective_id=0, has_side_effects=True, vmem_limit_bytes=60 * 1024 * 1024
        ),
        name="adjoint_steps",
    )(
        fringe_range,
        wind.reshape(3, tile, cz),
        adjoint.reshape(4, tile, cz),
        turbines.reshape(tile, cz),
    )
    return later.reshape(adjoint.shape)


def solution(mesh):
    in_specs = (
        P("dom", None, "gx", "gy", None),
        P("dom", None, "gx", "gy", None),
        P("gx", "gy", None),
        P(),
    )
    out_specs = P("dom", None, "gx", "gy", None)
    return jax.shard_map(
        on_device, mesh=mesh, in_specs=in_specs, out_specs=out_specs, check_vma=False
    )
```

```python
import functools
import math

import jax
import jax.numpy as jnp
from jax import lax
from jax.experimental import pallas as pl
from jax.experimental.pallas import tpu as pltpu
from jax.sharding import PartitionSpec as P

DT = 0.1
SMAG = 0.1
SOUND_SQ = 4.0
DRAG = 1.0
RATE = 3.0
H = 0.5 * DT
GROUP = 7


def shifted_z(field):
    depth = field.shape[-1]
    lane = lax.broadcasted_iota(jnp.int32, field.shape, 1)
    after = jnp.where(lane == depth - 1, 0.0, pltpu.roll(field, depth - 1, 1))
    before = jnp.where(lane == 0, 0.0, pltpu.roll(field, 1, 1))
    return after, before


def shifted_y(field, row_after=0.0, row_before=0.0):
    rows = field.shape[0]
    row = lax.broadcasted_iota(jnp.int32, field.shape, 0)
    after = jnp.where(row == rows - 1, row_after, pltpu.roll(field, rows - 1, 0))
    before = jnp.where(row == 0, row_before, pltpu.roll(field, 1, 0))
    return after, before


def kernel(
    sizes,
    fringe_hbm,
    wind,
    adjoint,
    turbines,
    out,
    a_ext,
    w_ext,
    n_ext,
    b_ext,
    turb,
    coef,
    a_in,
    w_in,
    n_in,
    b_in,
    a_out,
    w_out,
    b_out,
    corner_in,
    corner_out,
    w_row,
    first_main,
    second_main,
    rates,
    fringe,
    load_sem,
    send_sem,
    recv_sem,
):
    n_gx, n_gy, cells_x, cells_y = sizes
    cells_z = turb.shape[-1]
    dom, gx, gy = (lax.axis_index(a) for a in ("dom", "gx", "gy"))
    total = cells_x * n_gx
    reach = total // 4 - 1
    is_main = dom == 0
    in_fringe = jnp.logical_or(gx == n_gx - 1, gx * cells_x < reach)
    sends_forcing = jnp.logical_and(is_main, in_fringe)
    gets_forcing = jnp.logical_and(jnp.logical_not(is_main), in_fringe)
    up_x, down_x = lax.rem(gx + 1, n_gx), lax.rem(gx + n_gx - 1, n_gx)
    up_y, down_y = lax.rem(gy + 1, n_gy), lax.rem(gy + n_gy - 1, n_gy)
    places = ({"gx": up_x}, {"gx": down_x}, {"gy": up_y}, {"gy": down_y})
    partner = {"dom": 1 - dom}
    diagonal = tuple({"gx": x, "gy": y} for x in (up_x, down_x) for y in (up_y, down_y))

    def remote(src, dst, slot, device):
        return pltpu.make_async_remote_copy(
            src_ref=src,
            dst_ref=dst,
            send_sem=send_sem.at[slot],
            recv_sem=recv_sem.at[slot],
            device_id=device,
            device_id_type=pl.DeviceIdType.MESH,
        )

    inside = pl.ds(cells_y, cells_x * cells_y)
    inside_wind = pl.ds(2 * cells_y, cells_x * cells_y)
    load_fringe = pltpu.make_async_copy(fringe_hbm, fringe, load_sem.at[3])
    load_wind = pltpu.make_async_copy(wind, w_ext.at[:, inside_wind], load_sem.at[0])
    load_adjoint = pltpu.make_async_copy(adjoint, a_ext.at[:, inside], load_sem.at[1])
    load_turbines = pltpu.make_async_copy(turbines, turb, load_sem.at[2])

    barrier = pltpu.get_barrier_semaphore()
    for place in places + diagonal + (partner,):
        pl.semaphore_signal(
            barrier, inc=1, device_id=place, device_id_type=pl.DeviceIdType.MESH
        )
    load_wind.start()
    load_fringe.start()
    load_adjoint.start()
    load_turbines.start()
    pl.semaphore_wait(barrier, len(places) + len(diagonal) + 1)

    def slab(x):
        return pl.ds(pl.multiple_of(x * cells_y, 8), cells_y)

    def row(y, shift=0):
        return pl.ds(shift * cells_y + y, cells_x, stride=cells_y)

    def copies_x(slot, ext, last, first, depth):
        span = depth * cells_y
        pieces = (
            remote(last, ext.at[:, pl.ds(0, span)], slot, places[0]),
            remote(first, ext.at[:, pl.ds(cells_x * cells_y + span, span)], slot + 1, places[1]),
        )
        for piece in pieces:
            piece.start()
        return pieces

    def copies_y(slot, packed, sides):
        pieces = (
            remote(packed.at[0], sides.at[0], slot + 2, places[2]),
            remote(packed.at[1], sides.at[1], slot + 3, places[3]),
        )
        for piece in pieces:
            piece.start()
        return pieces

    span = 2 * cells_y
    wind_copies = copies_x(
        0,
        w_ext,
        wind.at[:, pl.ds((cells_x - 2) * cells_y, span)],
        wind.at[:, pl.ds(0, span)],
        2,
    )
    adjoint_copies = copies_x(
        4, a_ext, adjoint.at[:, slab(cells_x - 1)], adjoint.at[:, slab(0)], 1
    )
    load_wind.wait()
    for c in range(3):
        for j in range(2):
            w_out[0, c, j] = w_ext[c, row(cells_y - 1 - j, 2)]
            w_out[1, c, j] = w_ext[c, row(j, 2)]
    wind_copies += copies_y(0, w_out, w_in)
    load_adjoint.wait()
    for c in range(4):
        a_out[0, c] = a_ext[c, row(cells_y - 1, 1)]
        a_out[1, c] = a_ext[c, row(0, 1)]
    adjoint_copies += copies_y(4, a_out, a_in)
    corner_copies = []
    for q in range(4):
        x, y = (cells_x - 1, 0)[q // 2], (cells_y - 1, 0)[q % 2]
        for c in range(3):
            corner_out[q, c] = w_ext[c, pl.ds((x + 2) * cells_y + y, 1)]
        piece = remote(corner_out.at[q], corner_in.at[q], 8 + q, diagonal[q])
        piece.start()
        corner_copies.append(piece)
    first_forcing = remote(a_ext.at[pl.ds(0, 3), inside], first_main, 16, partner)

    @pl.when(sends_forcing)
    def _():
        first_forcing.start()

    def for_inner(body):
        inner = cells_x - 2
        size = max(g for g in range(1, GROUP + 1) if inner % g == 0)

        def several(i, carry):
            for k in range(size):
                body(1 + i * size + k)
            return carry

        lax.fori_loop(0, inner // size, several, 0)

    def for_slabs(body):
        body(0, lower=False)
        body(cells_x - 1, upper=False)
        for_inner(body)

    def neighbours(ext, c, x, lower=True, upper=True, base=1, rows=(0.0, 0.0)):
        here = ext[c, slab(x + base)]
        nothing = jnp.zeros_like(here)
        xp = ext[c, slab(x + base + 1)] if upper else nothing
        xm = ext[c, slab(x + base - 1)] if lower else nothing
        return (here, xp, xm, *shifted_y(here, *rows), *shifted_z(here))

    def strain(stencils):
        grads = []
        for _, xp, xm, yp, ym, zp, zm in stencils:
            grads.append((xp - xm, yp - ym, zp - zm))
        own = sum(grads[k][k] * grads[k][k] for k in range(3))
        xy = grads[0][1] + grads[1][0]
        xz = grads[0][2] + grads[2][0]
        yz = grads[1][2] + grads[2][1]
        return (0.5 * SMAG) * jnp.sqrt(2.0 * own + (xy * xy + xz * xz + yz * yz))

    def viscosity(x):
        n_ext[0, slab(x + 1)] = strain([neighbours(w_ext, c, x, base=2) for c in range(3)])

    for_inner(viscosity)
    for piece in wind_copies:
        piece.wait_recv()
    viscosity(0)
    viscosity(cells_x - 1)
    for side, y, inward in ((0, 0, 1), (1, cells_y - 1, cells_y - 2)):
        stencils = []
        for c in range(3):
            here, halo, near = w_ext[c, row(y, 2)], w_in[side, c, 0], w_ext[c, row(inward, 2)]
            along_y = (near, halo) if side == 0 else (halo, near)
            along_x = (w_ext[c, row(y, 3)], w_ext[c, row(y, 1)])
            stencils.append((here, *along_x, *along_y, *shifted_z(here)))
        n_ext[0, row(y, 1)] = strain(stencils)

    load_fringe.wait()
    position = gx * cells_x + lax.broadcasted_iota(jnp.int32, (cells_x, cells_z), 0)
    offset = position - fringe[0]
    offset = jnp.where(offset < 0, offset + total, offset)
    phase = math.pi * (offset.astype(jnp.float32) + 0.5) / fringe[1].astype(jnp.float32)
    sine = jnp.sin(phase)
    sign = jnp.where(is_main, -DT, DT)
    rates[...] = jnp.where(offset < fringe[1], sign * (RATE * sine * sine), 0.0)

    load_turbines.wait()
    drag_scale = jnp.where(is_main, DT * DRAG, 0.0)
    own_scale = jnp.where(is_main, 1.0, 0.0)

    def coefficients(x, **edges):
        u, v, w = (w_ext[c, slab(x + 2)] for c in range(3))
        nu, *faces = neighbours(n_ext, 0, x, **edges)
        nxp, nxm, nyp, nym, nzp, nzm = (face + nu for face in faces)
        speed = jnp.sqrt(u * u + v * v + w * w)
        drag = drag_scale * turb[slab(x)].astype(jnp.float32) * speed
        around = (nxp + nxm) + (nyp + nym) + (nzp + nzm)
        forcing = own_scale * rates[pl.ds(x, 1)]
        return (
            (1.0 + forcing) - H * around - drag,
            H * (nxp + u),
            H * (nxm - u),
            H * (nyp + v),
            H * (nym - v),
            H * (nzp + w),
            H * (nzm - w),
        )

    def advance(ext, weights, x, **edges):
        u, v, w = (w_ext[c, slab(x + 2)] for c in range(3))
        p, pxp, pxm, pyp, pym, pzp, pzm = neighbours(ext, 3, x, **edges)
        slopes = (pxp - pxm, pyp - pym, pzp - pzm)
        gain = u * slopes[0] + v * slopes[1] + w * slopes[2]
        results = []
        for c in range(3):
            stencil = neighbours(ext, c, x, **edges)
            gain = gain + (stencil[1 + 2 * c] - stencil[2 + 2 * c])
            new = sum(k * f for k, f in zip(weights, stencil))
            results.append(new + (SOUND_SQ * H) * slopes[c])
        results.append(p + H * gain)
        return results

    def first_step(x, **edges):
        weights = coefficients(x, **edges)
        for k, weight in enumerate(weights):
            coef[k, slab(x)] = weight
        for c, new in enumerate(advance(a_ext, weights, x, **edges)):
            b_ext[c, slab(x + 1)] = new

    for_slabs(first_step)

    @pl.when(gets_forcing)
    def _():
        first_forcing.wait_recv()

        def add(x, **_):
            rate = rates[pl.ds(x, 1)]
            for c in range(3):
                b_ext[c, slab(x + 1)] += rate * first_main[c, slab(x)]

        for_slabs(add)

    def of_side(side):
        return lambda ext, sides, c: sides[side, c]

    def of_slab(x):
        return lambda ext, sides, c: ext[c, slab(x)]

    layers = (
        (slab(0), slab(1), slab(2), of_slab(0), 2, 0, -1.0),
        (slab(cells_x - 1), slab(cells_x), slab(cells_x + 1), of_slab(cells_x + 1), 1, 0, 1.0),
        (row(0), row(0, 1), row(0, 2), of_side(0), 4, 1, -1.0),
        (row(cells_y - 1), row(cells_y - 1, 1), row(cells_y - 1, 2), of_side(1), 3, 1, 1.0),
    )

    def halo_terms(weight, velocity, layer, along, sign):
        terms = [weight * layer[c] for c in range(3)]
        terms[along] = terms[along] + (sign * SOUND_SQ * H) * layer[3]
        terms.append((sign * H) * (velocity * layer[3] + layer[along]))
        return terms

    for piece in corner_copies:
        piece.wait_recv()
    for x, q in ((-1, 0), (cells_x, 2)):
        n_ext[0, slab(x + 1)] = strain(
            [
                neighbours(w_ext, c, x, base=2, rows=(corner_in[q + 1, c], corner_in[q, c]))
                for c in range(3)
            ]
        )
    for side, y in ((0, 0), (1, cells_y - 1)):
        stencils = []
        for c in range(3):
            here, far, near = w_in[side, c, 0], w_in[side, c, 1], w_ext[c, row(y, 2)]
            w_row[side, c, pl.ds(8, cells_x)] = here
            w_row[side, c, pl.ds(7, 1)] = corner_in[side, c]
            w_row[side, c, pl.ds(8 + cells_x, 1)] = corner_in[2 + side, c]
            along_x = (w_row[side, c, pl.ds(9, cells_x)], w_row[side, c, pl.ds(7, cells_x)])
            along_y = (near, far) if side == 0 else (far, near)
            stencils.append((here, *along_x, *along_y, *shifted_z(here)))
        n_in[side, 0] = strain(stencils)

    for piece in adjoint_copies:
        piece.wait_recv()
    for place, extended, windy, layer_of, k, along, sign in layers:
        nu = H * layer_of(n_ext, n_in, 0)
        weight = coef[k, place] + nu
        coef[k, place] = weight
        coef[0, place] -= nu
        layer = [layer_of(a_ext, a_in, c) for c in range(4)]
        terms = halo_terms(weight, w_ext[along, windy], layer, along, sign)
        for c in range(4):
            new = b_ext[c, extended] + terms[c]
            if c < 3:
                new = new - nu * a_ext[c, extended]
            b_ext[c, extended] = new
            if along == 1:
                b_out[1 if sign < 0 else 0, c] = new
    second_copies = copies_y(12, b_out, b_in)
    second_copies += copies_x(12, b_ext, b_ext.at[:, slab(cells_x)], b_ext.at[:, slab(1)], 1)
    second_forcing = remote(b_ext.at[pl.ds(0, 3), inside], second_main, 17, partner)

    @pl.when(sends_forcing)
    def _():
        second_forcing.start()

    def second_step(x, **edges):
        weights = tuple(coef[k, slab(x)] for k in range(7))
        for c, new in enumerate(advance(b_ext, weights, x, **edges)):
            out[c, slab(x)] = new

    for_slabs(second_step)

    for piece in second_copies:
        piece.wait_recv()
    for place, extended, windy, layer_of, k, along, sign in layers:
        layer = [layer_of(b_ext, b_in, c) for c in range(4)]
        terms = halo_terms(coef[k, place], w_ext[along, windy], layer, along, sign)
        for c in range(4):
            out[c, place] += terms[c]

    @pl.when(gets_forcing)
    def _():
        second_forcing.wait_recv()

        def add(x, **_):
            rate = rates[pl.ds(x, 1)]
            for c in range(3):
                out[c, slab(x)] += rate * second_main[c, slab(x)]

        for_slabs(add)

    for piece in (*wind_copies, *corner_copies, *adjoint_copies, *second_copies):
        piece.wait_send()

    @pl.when(sends_forcing)
    def _():
        first_forcing.wait_send()
        second_forcing.wait_send()


def on_device(wind, adjoint, turbines, fringe_range):
    _, _, cx, cy, cz = wind.shape
    f32 = jnp.float32
    sizes = (lax.axis_size("gx"), lax.axis_size("gy"), cx, cy)
    around, tile, wide = (cx + 2) * cy, cx * cy, (cx + 4) * cy
    later = pl.pallas_call(
        functools.partial(kernel, sizes),
        out_shape=pltpu.VMEM((4, tile, cz), f32),
        in_specs=[pl.BlockSpec(memory_space=pltpu.HBM)] * 4,
        out_specs=pl.BlockSpec(memory_space=pltpu.VMEM),
        scratch_shapes=[
            pltpu.VMEM((4, around, cz), f32),
            pltpu.VMEM((3, wide, cz), f32),
            pltpu.VMEM((1, around, cz), f32),
            pltpu.VMEM((4, around, cz), f32),
            pltpu.VMEM((tile, cz), jnp.int32),
            pltpu.VMEM((7, tile, cz), f32),
            pltpu.VMEM((2, 4, cx, cz), f32),
            pltpu.VMEM((2, 3, 2, cx, cz), f32),
            pltpu.VMEM((2, 1, cx, cz), f32),
            pltpu.VMEM((2, 4, cx, cz), f32),
            pltpu.VMEM((2, 4, cx, cz), f32),
            pltpu.VMEM((2, 3, 2, cx, cz), f32),
            pltpu.VMEM((2, 4, cx, cz), f32),
            pltpu.VMEM((4, 3, 1, cz), f32),
            pltpu.VMEM((4, 3, 1, cz), f32),
            pltpu.VMEM((2, 3, cx + 16, cz), f32),
            pltpu.VMEM((3, tile, cz), f32),
            pltpu.VMEM((3, tile, cz), f32),
            pltpu.VMEM((cx, cz), f32),
            pltpu.SMEM((2,), jnp.int32),
            pltpu.SemaphoreType.DMA((4,)),
            pltpu.SemaphoreType.DMA((18,)),
            pltpu.SemaphoreType.DMA((18,)),
        ],
        compiler_params=pltpu.CompilerParams(
            collective_id=0, has_side_effects=True, vmem_limit_bytes=60 * 1024 * 1024
        ),
        name="adjoint_steps",
    )(
        fringe_range,
        wind.reshape(3, tile, cz),
        adjoint.reshape(4, tile, cz),
        turbines.reshape(tile, cz),
    )
    return later.reshape(adjoint.shape)


def solution(mesh):
    in_specs = (
        P("dom", None, "gx", "gy", None),
        P("dom", None, "gx", "gy", None),
        P("gx", "gy", None),
        P(),
    )
    out_specs = P("dom", None, "gx", "gy", None)
    return jax.shard_map(
        on_device, mesh=mesh, in_specs=in_specs, out_specs=out_specs, check_vma=False
    )
```
